128 devices in a mesh: group: 4 (over x), dev: 32 (over y, z, core).
Axes of the slice: x: 4, y: 4, z: 4, core: 2. Of those that a mesh axis runs over, the one named last changes fastest.
Arguments:
- embeddings: bfloat16 [131072, 768], P(('group', 'dev'))
- labels: int32 [131072], P(('group', 'dev')), may hold values from 0 to 4095, as said below
- ranking: int32 [131072], P(('group', 'dev')), may hold values from 0 to 131071, each once
- send_list: int32 [128, 32], P(('group', 'dev')), may hold values from 0 to 3
- pair_list: int32 [128, 32], P(('group', 'dev')), may hold values from 0 to 3
Outputs:
- scores: float32 [131072], P(('group', 'dev'))
- centroids: float32 [4096, 768], P(('group', 'dev'))
The draws below stay inside these ranges and needn't reach their ends.
Inputs may be any that keep to these rules, and one draw needn't show every extreme that they name: `labels`: every cluster holds at least one point, and cluster sizes are skewed. Within each group of 32 devices the points are sorted by cluster and laid out block by block: block k of the device with peer index d holds run number k * 32 + d of 256 points of the group in that order.
All inputs are finite; a program needn't handle non-finite values.
Results may differ from the reference program's by a relative error of at most 0.0003.
The reference program's roundings to bfloat16 on the way count: a program that leaves them out, or rounds other values in their place, can miss the bound.
Values may be sent and summed in bfloat16 or wider, within the bound.
A program may use at most 128 MiB of HBM per device.

```python
import jax
import jax.numpy as jnp
from jax import lax

D = 768
K = 4096
BLOCK = 256
NB = 4
P_DEV = 1024
POINTS = 131072
N_DEV = 32
DEVICES = 128


def cluster_labels(key):
    base_key = jax.random.fold_in(key, 11)
    group_total = DEVICES // N_DEV
    group_points = N_DEV * P_DEV
    heavy_points = group_points * 3 // 4
    light_points = group_points - heavy_points
    heavy_count = NB + 1
    shuffled = jax.random.permutation(jax.random.fold_in(base_key, 1), K).astype(jnp.int32)
    heavy_ids = shuffled[:group_total * heavy_count].reshape(group_total, heavy_count)
    first_pick = jax.random.randint(jax.random.fold_in(base_key, 2), (group_total, heavy_points), 0, heavy_count)
    second_pick = jax.random.randint(jax.random.fold_in(base_key, 3), (group_total, heavy_points), 0, heavy_count)
    heavy_rank = (first_pick * second_pick // (heavy_count - 1)).astype(jnp.int32)
    heavy_labels = jnp.take_along_axis(heavy_ids, heavy_rank, axis=1)
    light_labels = jax.random.randint(jax.random.fold_in(base_key, 4), (group_total * light_points,), 0, K).astype(jnp.int32)
    chosen_spots = jax.random.permutation(jax.random.fold_in(base_key, 5), group_total * light_points)[:K]
    light_labels = light_labels.at[chosen_spots].set(jnp.arange(K, dtype=jnp.int32))
    light_labels = light_labels.reshape(group_total, light_points)
    grouped = jnp.sort(jnp.concatenate([heavy_labels, light_labels], axis=1), axis=1)
    dealt_rows = grouped.reshape(group_total, NB, N_DEV, BLOCK).transpose(0, 2, 1, 3)
    return dealt_rows.reshape(POINTS).astype(jnp.int32)


def tile_lists(key):
    point_labels = cluster_labels(key)
    list_key = jax.random.fold_in(key, 21)
    group_total = DEVICES // N_DEV
    pair_count = NB * NB
    middle = point_labels.reshape(group_total, N_DEV, NB, BLOCK)[:, :, :, BLOCK // 2]
    matches = middle[:, :, None, :, None] == middle[:, None, :, None, :]
    matches = matches.reshape(group_total, N_DEV, N_DEV, pair_count)
    jitter = jax.random.randint(list_key, (group_total, N_DEV, N_DEV, pair_count), 0, 1024)
    ranked = matches.astype(jnp.int32) * (1024 * pair_count) + jitter * pair_count + jnp.arange(pair_count, dtype=jnp.int32)
    chosen_pair = lax.top_k(ranked, 1)[1][..., 0].astype(jnp.int32)
    sender_block = chosen_pair // NB
    receiver_block = chosen_pair % NB
    sent_blocks = sender_block.reshape(DEVICES, N_DEV).astype(jnp.int32)
    paired_blocks = receiver_block.transpose(0, 2, 1).reshape(DEVICES, N_DEV).astype(jnp.int32)
    return (sent_blocks, paired_blocks)


def partner_rows(key, point_labels, sent_blocks, paired_blocks):
    point_ids = jnp.arange(POINTS, dtype=jnp.int32)
    device_ids = point_ids // P_DEV
    block_ids = point_ids % P_DEV // BLOCK
    peer_ids = jax.random.randint(jax.random.fold_in(key, 7), (POINTS,), 0, N_DEV).astype(jnp.int32)
    sender_ids = device_ids // N_DEV * N_DEV + peer_ids
    tile_match = paired_blocks[device_ids, peer_ids] == block_ids
    sender_block = sent_blocks[sender_ids, device_ids % N_DEV]
    row_ids = jax.random.randint(jax.random.fold_in(key, 8), (POINTS,), 0, BLOCK).astype(jnp.int32)
    source_ids = (sender_ids * P_DEV + sender_block * BLOCK + row_ids).astype(jnp.int32)
    picked = jax.random.randint(jax.random.fold_in(key, 9), (POINTS,), 0, 100) < 16
    chosen = tile_match & picked & (point_labels[source_ids] == point_labels) & (sender_ids != device_ids)
    return (source_ids, chosen)


def draw_labels(key, part):
    return cluster_labels(key)


def draw_send_list(key, part):
    return tile_lists(key)[0]


def draw_pair_list(key, part):
    return tile_lists(key)[1]


def draw_embeddings(key, part):
    point_labels = cluster_labels(key)
    sent_blocks, paired_blocks = tile_lists(key)
    key = jax.random.fold_in(key, 5)
    center_table = jax.random.normal(jax.random.fold_in(key, 1), (K, D), jnp.float32)
    jitter = jax.random.normal(jax.random.fold_in(key, 2), (POINTS, D), jnp.float32)
    spread = jnp.exp(jax.random.uniform(jax.random.fold_in(key, 3), (POINTS, 1), jnp.float32, -0.7, 0.7))
    own_part = spread * jitter
    source_ids, chosen = partner_rows(key, point_labels, sent_blocks, paired_blocks)
    copy_noise = 0.05 * jax.random.normal(jax.random.fold_in(key, 6), (POINTS, D), jnp.float32)
    copied = own_part[source_ids] + copy_noise
    mixed = jnp.where(chosen[:, None], copied, own_part)
    return (center_table[point_labels] + mixed).astype(jnp.bfloat16)


def setup_inputs(seed: int = 0) -> dict:
    arg_keys = jax.random.split(jax.random.key(seed), 6)
    embeddings = draw_embeddings(jax.random.fold_in(arg_keys[5], 71), 0)
    labels = draw_labels(jax.random.fold_in(arg_keys[5], 71), 0)
    ranking = jax.random.permutation(arg_keys[2], POINTS).astype(jnp.int32)
    send_list = draw_send_list(jax.random.fold_in(arg_keys[5], 71), 0)
    pair_list = draw_pair_list(jax.random.fold_in(arg_keys[5], 71), 0)
    return {"embeddings": embeddings, "labels": labels, "ranking": ranking, "send_list": send_list, "pair_list": pair_list}


def make_unit(embeddings):
    values = embeddings.astype(jnp.float32)
    scaled = values * lax.rsqrt(lax.optimization_barrier(jnp.sum(values * values, axis=-1, keepdims=True)) + 1e-06)
    return scaled.astype(jnp.bfloat16)

def pair_best(left_rows, left_labels, left_ranks, right_rows, right_labels, right_ranks):
    similar = jnp.einsum('pjd,pid->pji', left_rows.astype(jnp.float32), right_rows.astype(jnp.float32), precision=lax.Precision.HIGHEST)
    same_label = left_labels[:, :, None] == right_labels[:, None, :]
    left_later = same_label & (right_ranks[:, None, :] < left_ranks[:, :, None])
    right_later = same_label & (left_ranks[:, :, None] < right_ranks[:, None, :])
    for_left = lax.optimization_barrier(jnp.max(jnp.where(left_later, similar, -2.0), axis=2))
    for_right = lax.optimization_barrier(jnp.max(jnp.where(right_later, similar, -2.0), axis=1))
    return (for_left, for_right)

def local_best(packed):
    rows, row_labels, row_ranks = packed
    similar = jnp.dot(rows, rows.T, preferred_element_type=jnp.float32)
    allowed = (row_labels[:, None] == row_labels[None, :]) & (row_ranks[None, :] < row_ranks[:, None])
    return lax.optimization_barrier(jnp.max(jnp.where(allowed, similar, -2.0), axis=1))

def reference(embeddings, labels, ranking, send_list, pair_list):
    unit_rows = make_unit(embeddings)
    device_count = send_list.shape[0]
    peer_count = send_list.shape[1]
    local_scores = lax.map(local_best, (unit_rows.reshape(device_count, P_DEV, D), labels.reshape(device_count, P_DEV), ranking.reshape(device_count, P_DEV)))
    blocks = unit_rows.reshape(device_count, NB, BLOCK, D)
    block_labels = labels.reshape(device_count, NB, BLOCK)
    block_ranks = ranking.reshape(device_count, NB, BLOCK)
    senders = jnp.broadcast_to(jnp.arange(device_count, dtype=jnp.int32)[:, None], (device_count, peer_count))
    receivers = senders // peer_count * peer_count + jnp.arange(peer_count, dtype=jnp.int32)[None, :]
    received_block = pair_list[receivers, senders % peer_count]

    def tile_pair(packed):
        sender_ids, sender_blocks, receiver_ids, receiver_blocks = packed
        return pair_best(blocks[sender_ids, sender_blocks], block_labels[sender_ids, sender_blocks], block_ranks[sender_ids, sender_blocks], blocks[receiver_ids, receiver_blocks], block_labels[receiver_ids, receiver_blocks], block_ranks[receiver_ids, receiver_blocks])
    for_sender, for_receiver = lax.map(tile_pair, (senders, send_list, receivers, received_block))
    best_seen = jnp.full((device_count, NB, BLOCK), -2.0, dtype=jnp.float32)
    best_seen = best_seen.at[senders, send_list].max(for_sender)
    best_seen = best_seen.at[receivers, received_block].max(for_receiver)
    scores = jnp.maximum(jnp.maximum(local_scores.reshape(-1), best_seen.reshape(-1)), 0.0)
    totals = jax.ops.segment_sum(unit_rows.astype(jnp.float32), labels, num_segments=K)
    centroids = totals * lax.rsqrt(lax.optimization_barrier(jnp.mean(totals * totals, axis=-1, keepdims=True)) + 1e-06)
    return (scores, centroids)
```

```python
import jax
import jax.numpy as jnp
from jax import lax
from jax.experimental import pallas as pl
from jax.experimental.pallas import tpu as pltpu
from jax.sharding import PartitionSpec as P

K = 4096
BLOCK = 256
ROWS = 1024
SLICES = 6
LANES = 128
LOW = -2.0
MESH = pl.DeviceIdType.MESH
M1, M2, M3, X1, X2, P0, P1, P2, P3 = range(9)
QUEUE = [("o", 0), ("o", 1), ("o", 2), ("o", 3), ("f", 0), ("f", 1), ("f", 2), ("f", 3), ("o", 4), ("o", 5), ("f", 4), ("f", 5),
         ("g", 0), ("g", 1), ("g", 2)]
ARRIVES = {"o": M1, "f": M2, "g": M3}


def pick(j, values):
    out = values[3]
    for i in (2, 1, 0):
        out = jnp.where(j == i, values[i], out)
    return out


def slice_id(j, n):
    pair = pick(j, ((2, 0, 1, 2), (0, 1, 0, 1), (1, 2, 2, 0))[n // 2])
    return pair * 2 + n % 2


def kernel(emb, lab_in, rank_in, send_in, pair_in, scores_out,
           own, m1, m2, m3, x1, x2, p0, p1, p2, p3,
           own_meta, *rest):
    metas = rest[0:9]
    lists = rest[9:19]
    cols = rest[19:27]
    accs = rest[27:37]
    flats = rest[37:47]
    (result_in, q_send, q_recv, fwd_send, fwd_recv, e_send, e_recv, d_send, d_recv, meta_send, meta_recv, list_sem,
     res_send, res_recv) = rest[47:]
    bufs = (m1, m2, m3, x1, x2, p0, p1, p2, p3)
    group = lax.axis_index("group")
    me = lax.axis_index("dev")
    core = lax.rem(me, 2)
    y, z = me // 8, lax.rem(me // 2, 4)
    main = jnp.where(core == 0, z, y)
    side = jnp.where(core == 0, y, z)
    phase = lax.rem(y + z, 4)

    def place(u, w, e):
        return lax.rem(u, 4) * (2 + 6 * e) + lax.rem(w, 4) * (8 - 6 * e) + e

    def at(index):
        return (group, index)

    other = 1 - core
    sources = [place(main + 1, side, core), place(main + 2, side, core), place(main + 3, side, core),
               place(main, side + 3, core), place(main, side + 2, core),
               place(side, main, other), place(side + 1, main, other), place(side + 2, main, other), place(side + 3, main, other)]
    holders = [place(main + 3, side, core), place(main + 2, side, core), place(main + 1, side, core),
               place(main, side + 1, core), place(main, side + 2, core),
               place(side, main, other), place(side, main + 3, other), place(side, main + 2, other), place(side, main + 1, other)]
    back = at(place(main + 3, side, core))
    forth = at(place(main + 1, side, core))
    along = at(place(main, side + 1, core))
    partner = at(place(side, main, other))

    barrier = pltpu.get_barrier_semaphore()

    def greet(i, carry):
        pl.semaphore_signal(barrier, inc=1, device_id=at(lax.rem(me + i, 32)), device_id_type=MESH)
        return carry

    lax.fori_loop(1, 32, greet, 0)

    own_meta[0:8, :] = lab_in[...]
    own_meta[8:16, :] = rank_in[...]
    own_meta[16:17, 0:32] = send_in[...]
    own_meta[17:18, 0:32] = pair_in[...]

    def normalize(i, carry):
        rows = pl.ds(pl.multiple_of(i * 128, 128), 128)
        values = emb[rows, :].astype(jnp.float32)
        scaled = values * lax.rsqrt(jnp.sum(values * values, axis=-1, keepdims=True) + 1e-06)
        unit = scaled.astype(jnp.bfloat16)
        for c in range(SLICES):
            own[c, i // 2, pl.ds(pl.multiple_of(lax.rem(i, 2) * 128, 128), 128), :] = unit[:, c * LANES:(c + 1) * LANES]
        return carry

    lax.fori_loop(0, 8, normalize, 0)
    pl.semaphore_wait(barrier, 31)

    started = []

    def remote(src, dst, send, recv, device):
        return pltpu.make_async_remote_copy(src_ref=src, dst_ref=dst, send_sem=send, recv_sem=recv, device_id=device,
                                            device_id_type=MESH)

    def go(copy):
        copy.start()
        started.append(copy)

    def queue_copy(k):
        kind, n = QUEUE[k]
        if kind == "o":
            c, src, dst = slice_id(phase, n), own, m1
        elif kind == "f":
            c, src, dst = slice_id(lax.rem(phase + 1, 4), n), m1, m2
        else:
            c, src, dst = slice_id(lax.rem(phase + 2, 4), n), m2, m3
        return remote(src.at[c], dst.at[c], q_send.at[k], q_recv.at[k], back)

    def queue_arrival(k):
        kind, n = QUEUE[k]
        if kind == "o":
            c, dst = slice_id(lax.rem(phase + 1, 4), n), m1
        elif kind == "f":
            c, dst = slice_id(lax.rem(phase + 2, 4), n), m2
        else:
            c, dst = slice_id(lax.rem(phase + 3, 4), n), m3
        return c, remote(dst.at[c], dst.at[c], q_send.at[k], q_recv.at[k], back)

    def forth_copy(i):
        c = slice_id(phase, i + 3)
        return remote(own.at[c], m3.at[c], fwd_send.at[i], fwd_recv.at[i], forth)

    def forth_arrival(i):
        c = slice_id(lax.rem(phase + 3, 4), i + 3)
        return c, remote(m3.at[c], m3.at[c], fwd_send.at[i], fwd_recv.at[i], forth)

    def side_copy(k):
        if k < 6:
            return remote(own.at[k], x1.at[k], e_send.at[k], e_recv.at[k], along)
        return remote(x1.at[k - 6], x2.at[k - 6], e_send.at[k], e_recv.at[k], along)

    def side_arrival(k):
        dst = x1.at[k] if k < 6 else x2.at[k - 6]
        return remote(dst, dst, e_send.at[k], e_recv.at[k], along)

    go(queue_copy(0))
    go(forth_copy(1))
    go(side_copy(0))
    go(queue_copy(1))
    go(forth_copy(2))
    go(side_copy(1))
    for i in range(9):
        go(remote(own_meta, metas[i], meta_send.at[i], meta_recv.at[i], at(holders[i])))
    go(remote(own, p0, d_send.at[0], d_recv.at[0], partner))

    shares = [0]

    def share(which, c):
        shares[0] += 1
        src, dst = bufs[which], bufs[which + P1]
        go(remote(src.at[c], dst.at[c], d_send.at[shares[0]], d_recv.at[which + 1], partner))

    def shared_arrival(i):
        dst = (p0, p1, p2, p3)[i]
        remote(dst, dst, d_send.at[0], d_recv.at[i], partner).wait_recv()

    def make_cols(meta, i):
        for part in range(2):
            for r in range(8):
                row = jnp.broadcast_to(meta[part * 8 + r:part * 8 + r + 1, :], (LANES, LANES))
                cols[2 * i + part][r // 2, (r % 2) * LANES:(r % 2 + 1) * LANES, :] = row.T

    def make_rows(meta, i):
        for part in range(2):
            for r in range(8):
                flats[i][r // 2, part:part + 1, (r % 2) * LANES:(r % 2 + 1) * LANES] = meta[part * 8 + r:part * 8 + r + 1, :]

    make_cols(own_meta, 0)
    make_rows(own_meta, 9)
    own_list = pltpu.make_async_copy(own_meta.at[pl.ds(16, 8)], lists[9], list_sem.at[9])
    own_list.start()
    for acc in accs:
        acc[...] = jnp.full((8, LANES), LOW, jnp.float32)
    row_ids = lax.broadcasted_iota(jnp.int32, (8, LANES), 0)

    def update(acc, block, row):
        spread = jnp.where(lax.rem(row_ids, 2) == 0, row[:, :LANES], row[:, LANES:])
        acc[...] = jnp.where(row_ids // 2 == block, jnp.maximum(acc[...], spread), acc[...])

    def tile(abuf, acol, aacc, a, bbuf, brows, bacc, b, same=False):
        left = jnp.concatenate([abuf[c, a] for c in range(SLICES)], axis=1)
        right = jnp.concatenate([bbuf[c, b] for c in range(SLICES)], axis=1)
        similar = lax.dot_general(left, right, (((1,), (1,)), ((), ())), preferred_element_type=jnp.float32)
        alab, arank = cols[2 * acol][a], cols[2 * acol + 1][a]
        brow = brows[b]
        for_a, for_b = None, []
        for h in range(2):
            blab = brow[0:1, h * LANES:(h + 1) * LANES]
            brank = brow[1:2, h * LANES:(h + 1) * LANES]
            value = jnp.where(alab == blab, similar[:, h * LANES:(h + 1) * LANES], LOW)
            later = brank < arank
            va = jnp.where(later, value, LOW)
            vb = jnp.where(arank < brank, value, LOW) if same else jnp.where(later, LOW, value)
            for_a = va if for_a is None else jnp.maximum(for_a, va)
            for_b.append(jnp.max(vb, axis=0, keepdims=True))
        update(aacc, a, jnp.max(for_a.T, axis=0, keepdims=True))
        update(bacc, b, jnp.concatenate(for_b, axis=1))

    def data(i):
        if i is None:
            return own, flats[9], lists[9], accs[9], me
        return bufs[i], flats[i], lists[i], accs[i], sources[i]

    def meet(ai, bi, forward=True, backward=True):
        abuf, _, alist, aacc, adev = data(ai)
        bbuf, brows, blist, bacc, bdev = data(bi)
        col = 0 if ai is None else ai + 1

        def one(i, carry):
            sends = i == 0
            a = jnp.where(sends, alist[0, bdev], alist[1, bdev])
            b = jnp.where(sends, blist[1, adev], blist[0, adev])
            tile(abuf, col, aacc, a, bbuf, brows, bacc, b)
            return carry

        lax.fori_loop(0 if forward else 1, 2 if backward else 1, one, 0)

    def local(lo, hi):
        def one(i, carry):
            k = jnp.where(i >= 4, 1, 0) + jnp.where(i >= 7, 1, 0) + jnp.where(i >= 9, 1, 0)
            l = i - pick(k, (0, 3, 5, 6))
            tile(own, 0, accs[9], k, own, flats[9], accs[9], l, same=True)
            return carry

        lax.fori_loop(lo, hi, one, 0)

    def have_meta(i):
        remote(metas[i], metas[i], meta_send.at[i], meta_recv.at[i], partner).wait_recv()
        copy = pltpu.make_async_copy(metas[i].at[pl.ds(16, 8)], lists[i], list_sem.at[i])
        copy.start()
        return copy

    def give_back(i):
        go(remote(accs[i], result_in.at[i], res_send.at[i], res_recv.at[i], at(sources[i])))

    local(0, 4)
    for k in range(15):
        c, copy = queue_arrival(k)
        copy.wait_recv()
        if k + 2 < 15:
            go(queue_copy(k + 2))
        share(ARRIVES[QUEUE[k][0]], c)
        if 2 <= k < 14:
            side_arrival(k - 2).wait_recv()
            if k < 12:
                go(side_copy(k))
        if k == 1:
            pending = [have_meta(i) for i in range(9)]
            for copy in pending:
                copy.wait()
            own_list.wait()
            for i in range(9):
                make_rows(metas[i], i)
            for i in range(3):
                make_cols(metas[i], i + 1)
        if k == 0:
            local(4, 10)
        if k == 2:
            shared_arrival(0)
            meet(None, P0, backward=False)
        if k == 3:
            for i in (1, 2):
                c, copy = forth_arrival(i)
                copy.wait_recv()
                share(M3, c)
        if k == 6:
            go(forth_copy(0))
        if k == 7:
            meet(None, X1)
        if k == 9:
            meet(None, M1)
            meet(M1, X1)
            meet(M1, P0, backward=False)
        if k == 10:
            shared_arrival(1)
            meet(None, P1, backward=False)
            meet(M1, P1, backward=False)
        if k == 11:
            meet(None, M2, forward=False)
            meet(M2, X1)
            meet(M2, P0, backward=False)
            meet(M2, P1, backward=False)
        if k == 12:
            shared_arrival(2)
            meet(None, P2, backward=False)
            meet(M1, P2, backward=False)
            meet(M2, P2, backward=False)
            c, copy = forth_arrival(0)
            copy.wait_recv()
            share(M3, c)
        if k == 13:
            meet(None, X2, forward=False)
            meet(M1, X2, forward=False)
            meet(M2, X2, forward=False)
            for i in (P0, P1):
                pass
    meet(M3, X2, forward=False)
    give_back(X2)
    meet(M3, X1)
    give_back(X1)
    meet(M3, P0, backward=False)
    give_back(P0)
    meet(M3, P1, backward=False)
    give_back(P1)
    meet(M3, P2, backward=False)
    give_back(P2)
    shared_arrival(3)
    meet(M3, P3, backward=False)
    give_back(M3)
    meet(M2, P3, backward=False)
    give_back(M2)
    meet(M1, P3, backward=False)
    give_back(M1)
    meet(None, P3, backward=False)
    give_back(P3)

    best = jnp.maximum(accs[9][...], 0.0)
    for i in range(9):
        remote(result_in.at[i], result_in.at[i], res_send.at[i], res_recv.at[i], partner).wait_recv()
        best = jnp.maximum(best, result_in[i])
    scores_out[...] = best
    for copy in started:
        copy.wait_send()


def exchange(embeddings, labels, ranking, send_list, pair_list):
    dataset = pltpu.VMEM((SLICES, 4, BLOCK, LANES), jnp.bfloat16)
    dma = pltpu.SemaphoreType.DMA
    return pl.pallas_call(
        kernel,
        out_shape=jax.ShapeDtypeStruct((8, LANES), jnp.float32),
        in_specs=[pl.BlockSpec(memory_space=pltpu.VMEM)] * 5,
        out_specs=pl.BlockSpec(memory_space=pltpu.VMEM),
        scratch_shapes=[dataset] * 10
        + [pltpu.VMEM((24, LANES), jnp.int32)] * 10
        + [pltpu.SMEM((8, LANES), jnp.int32)] * 10
        + [pltpu.VMEM((4, BLOCK, LANES), jnp.int32)] * 8
        + [pltpu.VMEM((8, LANES), jnp.float32)] * 10
        + [pltpu.VMEM((4, 8, BLOCK), jnp.int32)] * 10
        + [pltpu.VMEM((9, 8, LANES), jnp.float32),
           dma((15,)), dma((15,)), dma((3,)), dma((3,)), dma((12,)), dma((12,)), dma((20,)), dma((4,)),
           dma((9,)), dma((9,)), dma((10,)), dma((9,)), dma((9,))],
        compiler_params=pltpu.CompilerParams(collective_id=0, has_side_effects=True, vmem_limit_bytes=56 * 1024 * 1024),
    )(embeddings, labels.reshape(8, LANES), ranking.reshape(8, LANES), send_list, pair_list)


def body(embeddings, labels, ranking, send_list, pair_list):
    scores = exchange(embeddings, labels, ranking, send_list, pair_list).reshape(ROWS)
    values = embeddings.astype(jnp.float32)
    unit_rows = (values * lax.rsqrt(jnp.sum(values * values, axis=-1, keepdims=True) + 1e-06)).astype(jnp.bfloat16)
    cluster_ids = jnp.arange(K, dtype=jnp.int32)
    indicator = (cluster_ids[:, None] == labels[None, :]).astype(jnp.bfloat16)
    totals = lax.psum_scatter(
        jnp.dot(indicator, unit_rows, preferred_element_type=jnp.float32),
        ("group", "dev"),
        scatter_dimension=0,
        tiled=True,
    )
    centroids = totals * lax.rsqrt(jnp.mean(totals * totals, axis=-1, keepdims=True) + 1e-06)
    return (scores, centroids)


def solution(mesh):
    return jax.shard_map(
        body,
        mesh=mesh,
        in_specs=(
            P(("group", "dev"), None),
            P(("group", "dev")),
            P(("group", "dev")),
            P(("group", "dev"), None),
            P(("group", "dev"), None),
        ),
        out_specs=(P(("group", "dev")), P(("group", "dev"), None)),
        check_vma=False,
    )
```

```python
import jax
import jax.numpy as jnp
from jax import lax
from jax.experimental import pallas as pl
from jax.experimental.pallas import tpu as pltpu
from jax.sharding import PartitionSpec as P

K = 4096
BLOCK = 256
ROWS = 1024
SLICES = 6
LANES = 128
LOW = -2.0
MESH = pl.DeviceIdType.MESH
WINDOW = 4
M1, M2, M3, X1, X2, P0, P1, P2, P3 = range(9)
QUEUE = ([("o", n) for n in range(6)] + [("f", n) for n in range(6)] + [("g", n) for n in range(3)])


def kernel(emb, lab_in, rank_in, send_in, pair_in, scores_out, centroids_out,
           own, m1, m2, m3, x1, x2, p0, p1, p2, p3, *rest):
    metas = rest[0:10]
    lists = rest[10:20]
    cols = rest[20:28]
    accs = rest[28:38]
    flats = rest[38:48]
    own_meta = metas[9]
    (result_in, halves, xa, xp, xmeta, rhs, ids_row, ids_side, sums, cores, from_core, in_f, in_b, in2_f, in2_b, in_side, in_x,
     q_send, q_recv, fwd_send, fwd_recv, e_send, e_recv, d_send, d_recv, meta_send, meta_recv, list_sem, res_send, res_recv,
     x_send, x_recv, c_send, c_recv) = rest[48:]
    bufs = (m1, m2, m3, x1, x2, p0, p1, p2, p3)
    group = lax.axis_index("group")
    me = lax.axis_index("dev")
    core = lax.rem(me, 2)
    y, z = me // 8, lax.rem(me // 2, 4)
    main = jnp.where(core == 0, z, y)
    side = jnp.where(core == 0, y, z)
    def place(u, w, e):
        return lax.rem(u, 4) * (2 + 6 * e) + lax.rem(w, 4) * (8 - 6 * e) + e

    def at(index):
        return (group, index)

    other = 1 - core
    sources = [place(main + 1, side, core), place(main + 2, side, core), place(main + 3, side, core),
               place(main, side + 3, core), place(main, side + 2, core),
               place(side, main, other), place(side + 1, main, other), place(side + 2, main, other), place(side + 3, main, other)]
    back = at(place(main + 3, side, core))
    forth = at(place(main + 1, side, core))
    along = at(place(main, side + 1, core))
    partner = at(place(side, main, other))

    behind = at(place(main, side + 3, core))
    across = at(place(main, side + 2, core))
    mates = [(lax.rem(group + i, 4), me) for i in (1, 2, 3)]

    barrier = pltpu.get_barrier_semaphore()
    for device in [forth, back, along, behind, partner] + mates:
        pl.semaphore_signal(barrier, inc=1, device_id=device, device_id_type=MESH)

    own_meta[0:8, :] = lab_in[...]
    own_meta[8:16, :] = rank_in[...]
    own_meta[16:17, 0:32] = send_in[...]
    own_meta[17:18, 0:32] = pair_in[...]

    def normalize(i, carry):
        rows = pl.ds(pl.multiple_of(i * 128, 128), 128)
        values = emb[rows, :].astype(jnp.float32)
        scaled = values * lax.rsqrt(jnp.sum(values * values, axis=-1, keepdims=True) + 1e-06)
        unit = scaled.astype(jnp.bfloat16)
        for c in range(SLICES):
            own[c, i // 2, pl.ds(pl.multiple_of(lax.rem(i, 2) * 128, 128), 128), :] = unit[:, c * LANES:(c + 1) * LANES]
        return carry

    lax.fori_loop(0, 8, normalize, 0)
    lane_ids = lax.broadcasted_iota(jnp.int32, (BLOCK, LANES), 1)

    for t in range(2):
        for b in range(2):
            low = own[4 + t, b].astype(jnp.float32)
            high = own[4 + t, b + 2].astype(jnp.float32)
            halves[2 * t, b] = jnp.where(lane_ids < 64, low, pltpu.roll(high, 64, 1)).astype(jnp.bfloat16)
            halves[2 * t + 1, b] = jnp.where(lane_ids < 64, pltpu.roll(low, 64, 1), high).astype(jnp.bfloat16)
    pl.semaphore_wait(barrier, 8)

    started = []

    def remote(src, dst, send, recv, device):
        return pltpu.make_async_remote_copy(src_ref=src, dst_ref=dst, send_sem=send, recv_sem=recv, device_id=device,
                                            device_id_type=MESH)

    def go(copy):
        copy.start()
        started.append(copy)

    rings = {"o": (own, m1), "f": (m1, m2), "g": (m2, m3)}

    def queue_copy(k):
        kind, n = QUEUE[k]
        src, dst = rings[kind]
        return remote(src.at[n], dst.at[n], q_send.at[k], q_recv.at[k], back)

    def forth_copy(i):
        return remote(own.at[i + 3], m3.at[i + 3], fwd_send.at[i], fwd_recv.at[i], forth)

    def side_copy(k):
        if k < 6:
            return remote(own.at[k], x1.at[k], e_send.at[k], e_recv.at[k], along)
        return remote(x1.at[k - 6], x2.at[k - 6], e_send.at[k], e_recv.at[k], along)

    def side_arrival(k):
        dst = x1.at[k] if k < 6 else x2.at[k - 6]
        return remote(dst, dst, e_send.at[k], e_recv.at[k], along)

    meta_routes = [(9, M1, back), (9, M3, forth), (9, X1, along), (9, P0, partner),
                   (M1, M2, back), (X1, X2, along), (M1, P1, partner), (M3, P3, partner), (M2, P2, partner)]

    def meta_go(i):
        src, dst, device = meta_routes[i]
        go(remote(metas[src], metas[dst], meta_send.at[i], meta_recv.at[dst], device))

    def mate_copies(i):
        quarter = lax.rem(group + 1 + i, 4)
        go(remote(own_meta.at[pl.ds(0, 8)], xmeta.at[i], x_send.at[i, 0], x_recv.at[i, 0], mates[i]))
        go(remote(own.at[quarter], xa.at[i], x_send.at[i, 1], x_recv.at[i, 1], mates[i]))
        go(remote(halves.at[quarter], xp.at[i], x_send.at[i, 2], x_recv.at[i, 2], mates[i]))

    go(queue_copy(0))
    go(side_copy(0))
    mate_copies(0)
    mate_copies(2)
    for i in range(4):
        meta_go(i)
    go(queue_copy(1))
    go(side_copy(1))
    go(remote(own, p0, d_send.at[0], d_recv.at[0], partner))
    mate_copies(1)
    for k in range(2, WINDOW):
        go(queue_copy(k))
        go(side_copy(k))

    def share(which, first, count, slot):
        src, dst = bufs[which], bufs[which + P1]
        go(remote(src.at[pl.ds(first, count)], dst.at[pl.ds(first, count)], d_send.at[slot], d_recv.at[which + 1], partner))

    def shared_arrival(i):
        dst = (p0, p1, p2, p3)[i]
        remote(dst, dst, d_send.at[0], d_recv.at[i], partner).wait_recv()

    def landed(dst, recv):
        remote(dst, dst, res_send.at[0], recv, partner).wait_recv()

    def make_cols(meta, i):
        for part in range(2):
            for r in range(8):
                row = jnp.broadcast_to(meta[part * 8 + r:part * 8 + r + 1, :], (LANES, LANES))
                cols[2 * i + part][r // 2, (r % 2) * LANES:(r % 2 + 1) * LANES, :] = row.T

    def make_rows(meta, i):
        for part in range(2):
            for r in range(8):
                flats[i][r // 2, part:part + 1, (r % 2) * LANES:(r % 2 + 1) * LANES] = meta[part * 8 + r:part * 8 + r + 1, :]

    make_cols(own_meta, 0)
    make_rows(own_meta, 9)
    own_list = pltpu.make_async_copy(own_meta.at[pl.ds(16, 8)], lists[9], list_sem.at[9])
    own_list.start()
    for acc in accs:
        acc[...] = jnp.full((8, LANES), LOW, jnp.float32)
    row_ids = lax.broadcasted_iota(jnp.int32, (8, LANES), 0)

    def update(acc, block, row):
        spread = jnp.where(lax.rem(row_ids, 2) == 0, row[:, :LANES], row[:, LANES:])
        acc[...] = jnp.where(row_ids // 2 == block, jnp.maximum(acc[...], spread), acc[...])

    def tile(abuf, acol, aacc, a, bbuf, brows, bacc, b, same=False):
        left = jnp.concatenate([abuf[c, a] for c in range(SLICES)], axis=1)
        right = jnp.concatenate([bbuf[c, b] for c in range(SLICES)], axis=1)
        similar = lax.dot_general(left, right, (((1,), (1,)), ((), ())), preferred_element_type=jnp.float32)
        alab, arank = cols[2 * acol][a], cols[2 * acol + 1][a]
        brow = brows[b]
        for_a, for_b = None, []
        for h in range(2):
            blab = brow[0:1, h * LANES:(h + 1) * LANES]
            brank = brow[1:2, h * LANES:(h + 1) * LANES]
            value = jnp.where(alab == blab, similar[:, h * LANES:(h + 1) * LANES], LOW)
            later = brank < arank
            va = jnp.where(later, value, LOW)
            vb = jnp.where(arank < brank, value, LOW) if same else jnp.where(later, LOW, value)
            for_a = va if for_a is None else jnp.maximum(for_a, va)
            for_b.append(jnp.max(vb, axis=0, keepdims=True))
        update(aacc, a, jnp.max(for_a.T, axis=0, keepdims=True))
        update(bacc, b, jnp.concatenate(for_b, axis=1))

    def data(i):
        if i is None:
            return own, flats[9], lists[9], accs[9], me
        return bufs[i], flats[i], lists[i], accs[i], sources[i]

    def meet(ai, bi, forward=True, backward=True):
        abuf, _, alist, aacc, adev = data(ai)
        bbuf, brows, blist, bacc, bdev = data(bi)
        col = 0 if ai is None else ai + 1

        def one(i, carry):
            sends = i == 0
            a = jnp.where(sends, alist[0, bdev], alist[1, bdev])
            b = jnp.where(sends, blist[1, adev], blist[0, adev])
            tile(abuf, col, aacc, a, bbuf, brows, bacc, b)
            return carry

        lax.fori_loop(0 if forward else 1, 2 if backward else 1, one, 0)

    def local(lo, hi):
        def one(i, carry):
            k = jnp.where(i >= 4, 1, 0) + jnp.where(i >= 7, 1, 0) + jnp.where(i >= 9, 1, 0)
            l = i - 3 * jnp.where(i >= 4, 1, 0) - 2 * jnp.where(i >= 7, 1, 0) - jnp.where(i >= 9, 1, 0)
            tile(own, 0, accs[9], k, own, flats[9], accs[9], l, same=True)
            return carry

        lax.fori_loop(lo, hi, one, 0)

    def have_meta(i):
        landed(metas[i], meta_recv.at[i])

    def use_meta(i):
        copy = pltpu.make_async_copy(metas[i].at[pl.ds(16, 8)], lists[i], list_sem.at[i])
        copy.start()
        make_rows(metas[i], i)
        if i < 3:
            make_cols(metas[i], i + 1)
        copy.wait()

    rows_iota = lax.broadcasted_iota(jnp.int32, (BLOCK, LANES), 0)
    ids_row[...] = lax.rem(rows_iota // 32, 4) * 1024 + lax.rem(rows_iota, 32)
    ids_side[...] = rows_iota // 128

    def set_source(points, extra):
        for b in range(4):
            rhs[b * BLOCK:(b + 1) * BLOCK, :LANES] = points[b]
            keep = (lane_ids < 64) if b < 2 else (lane_ids >= 64)
            rhs[b * BLOCK:(b + 1) * BLOCK, LANES:] = jnp.where(keep, extra[b % 2].astype(jnp.float32), 0.0).astype(jnp.bfloat16)

    def add_source(labels, lo, hi, mode):
        def chunk(i, carry):
            m = lax.rem(i + 8 * other, 16)
            e1, m1_, h = m // 8, lax.rem(m // 2, 4), lax.rem(m, 2)
            step = 256 - 192 * e1
            base = e1 * 32 + m1_ * (64 + 192 * e1) + 2 * h * step
            ids = ids_row[...] + ids_side[...] * step + base
            hot = jnp.concatenate(
                [jnp.where(labels[r:r + 1, :] == ids, 1.0, 0.0).astype(jnp.bfloat16) for r in range(8)], axis=1)
            total = jnp.dot(hot, rhs[...], preferred_element_type=jnp.float32)
            if mode != "first":
                total = total + sums[m]
            if mode != "last":
                sums[m] = total
            else:
                extra = total[:, LANES:]
                extra = extra + pltpu.roll(extra, 64, 1)
                for b in range(8):
                    rows = slice(b * 32, b * 32 + 32)
                    cores[e1, m1_, 2 * h + b // 4, b % 4, 0:32, :] = total[rows, :LANES]
                    cores[e1, m1_, 2 * h + b // 4, b % 4, 32:48, :] = jnp.where(
                        lane_ids[:16] < 64, extra[b * 32:b * 32 + 16], extra[b * 32 + 16:b * 32 + 32])
            return carry

        lax.fori_loop(lo, hi, chunk, 0)

    def ring(i):
        return lax.rem(main + i, 4)

    def centroid_send(src, dst, i, device):
        go(remote(src, dst, c_send.at[i], c_recv.at[i], device))

    def finish_centroids():
        quarters = [in_x[lax.rem(group - q + 4, 4)] for q in range(4)]
        tiles = [quarters[q][0:32] for q in range(4)]
        low = lane_ids[:16] < 64
        for t in range(2):
            even, odd = quarters[2 * t][32:48], quarters[2 * t + 1][32:48]
            tiles.append(jnp.concatenate([jnp.where(low, even, pltpu.roll(odd, 64, 1)),
                                          jnp.where(low, pltpu.roll(even, 64, 1), odd)], axis=0))
        squares = tiles[0] * tiles[0]
        for tile_values in tiles[1:]:
            squares = squares + tile_values * tile_values
        scale = lax.rsqrt(jnp.sum(squares, axis=-1, keepdims=True) / 768.0 + 1e-06)
        for c in range(SLICES):
            centroids_out[:, c * LANES:(c + 1) * LANES] = tiles[c] * scale

    def give_back(i):
        go(remote(accs[i], result_in.at[i], res_send.at[i], res_recv.at[i], at(sources[i])))

    def source(i):
        landed(xmeta.at[i], x_recv.at[i, 0])
        landed(xa.at[i], x_recv.at[i, 1])
        landed(xp.at[i], x_recv.at[i, 2])
        set_source(xa.at[i], xp.at[i])

    own_list.wait()
    local(0, 3)
    for k in range(15):
        kind, n = QUEUE[k]
        landed(rings[kind][1].at[n], q_recv.at[k])
        if k + WINDOW < 15:
            go(queue_copy(k + WINDOW))
        if 2 <= k < 14:
            dst = x1.at[k - 2] if k < 8 else x2.at[k - 8]
            landed(dst, e_recv.at[k - 2])
            if k - 2 + WINDOW < 12:
                go(side_copy(k - 2 + WINDOW))
        if k == 0:
            have_meta(M1)
            meta_go(4)
            meta_go(6)
            have_meta(X1)
            meta_go(5)
            have_meta(M3)
            meta_go(7)
            have_meta(P0)
            local(3, 6)
        if k == 1:
            have_meta(M2)
            meta_go(8)
            for i in (M1, M3, X1, P0, M2):
                use_meta(i)
            local(6, 10)
        if k == 2:
            for i in (X2, P1, P2, P3):
                have_meta(i)
                use_meta(i)
            set_source(own.at[group], halves.at[group])
            add_source(own_meta, 0, 8, "first")
        if k == 3:
            add_source(own_meta, 8, 16, "first")
        if 3 <= k < 6:
            go(forth_copy(k - 3))
        if k == 4:
            shared_arrival(0)
            meet(None, P0, backward=False)
        if k == 5:
            share(M1, 0, 6, 1)
            meet(None, M1)
            meet(M1, P0, backward=False)
        if k == 6:
            source(0)
            add_source(xmeta.at[0], 0, 16, "add")
        if k == 7:
            source(2)
            add_source(xmeta.at[2], 0, 16, "add")
        if k == 8:
            source(1)
            add_source(xmeta.at[1], 0, 8, "last")
            centroid_send(cores.at[other], from_core, 0, partner)
            add_source(xmeta.at[1], 8, 16, "last")
        if k == 9:
            meet(None, X1)
            meet(M1, X1)
            landed(from_core, c_recv.at[0])
            for i in range(4):
                cores[core, i] = cores[core, i] + from_core[i]
            centroid_send(cores.at[core, ring(2), pl.ds(0, 2)], in_f, 1, forth)
            centroid_send(cores.at[core, ring(2), pl.ds(2, 2)], in_b, 2, back)
        if k == 10:
            shared_arrival(1)
            meet(None, P1, backward=False)
            meet(M1, P1, backward=False)
            landed(in_f, c_recv.at[1])
            cores[core, ring(1), 0:2] = cores[core, ring(1), 0:2] + in_f[...]
            centroid_send(cores.at[core, ring(1)], in2_f, 3, forth)
            landed(in_b, c_recv.at[2])
            cores[core, ring(3), 2:4] = cores[core, ring(3), 2:4] + in_b[...]
            centroid_send(cores.at[core, ring(3)], in2_b, 4, back)
        if k == 11:
            share(M2, 0, 6, 2)
            meet(None, M2, forward=False)
            meet(M2, X1)
            meet(M2, P0, backward=False)
            meet(M2, P1, backward=False)
        if k == 12:
            for i in range(3):
                landed(m3.at[i + 3], fwd_recv.at[i])
            share(M3, 3, 3, 3)
            landed(in2_f, c_recv.at[3])
            landed(in2_b, c_recv.at[4])
            cores[core, main] = cores[core, main] + in2_f[...] + in2_b[...]
            for i, device in ((1, along), (2, across), (3, behind)):
                centroid_send(cores.at[core, main, lax.rem(side + i, 4)], in_side.at[i], 4 + i, device)
            shared_arrival(2)
            meet(None, P2, backward=False)
            meet(M1, P2, backward=False)
            meet(M2, P2, backward=False)
        if k == 13:
            share(M3, 0, 2, 4)
            meet(None, X2, forward=False)
            meet(M1, X2, forward=False)
            meet(M2, X2, forward=False)
    share(M3, 2, 1, 5)
    for i in (1, 2, 3):
        landed(in_side.at[i], c_recv.at[4 + i])
    in_side[0] = cores[core, main, side] + in_side[1] + in_side[2] + in_side[3]
    in_x[0] = in_side[0, group]
    for i in (1, 2, 3):
        centroid_send(in_side.at[0, lax.rem(group + i, 4)], in_x.at[i], 7 + i, mates[i - 1])
    meet(M3, X2, forward=False)
    give_back(X2)
    meet(M3, X1)
    give_back(X1)
    meet(M3, P0, backward=False)
    give_back(P0)
    meet(M3, P1, backward=False)
    give_back(P1)
    meet(M3, P2, backward=False)
    give_back(P2)
    shared_arrival(3)
    meet(M3, P3, backward=False)
    give_back(M3)
    meet(M2, P3, backward=False)
    give_back(M2)
    meet(M1, P3, backward=False)
    give_back(M1)
    meet(None, P3, backward=False)
    give_back(P3)

    for i in (1, 2, 3):
        landed(in_x.at[i], c_recv.at[7 + i])
    finish_centroids()
    best = jnp.maximum(accs[9][...], 0.0)
    for i in range(9):
        remote(result_in.at[i], result_in.at[i], res_send.at[i], res_recv.at[i], partner).wait_recv()
        best = jnp.maximum(best, result_in[i])
    scores_out[...] = best
    for copy in started:
        copy.wait_send()


def exchange(embeddings, labels, ranking, send_list, pair_list):
    dataset = pltpu.VMEM((SLICES, 4, BLOCK, LANES), jnp.bfloat16)
    dma = pltpu.SemaphoreType.DMA
    f32, bf16, i32 = jnp.float32, jnp.bfloat16, jnp.int32
    return pl.pallas_call(
        kernel,
        out_shape=(jax.ShapeDtypeStruct((8, LANES), f32), jax.ShapeDtypeStruct((32, SLICES * LANES), f32)),
        in_specs=[pl.BlockSpec(memory_space=pltpu.VMEM)] * 5,
        out_specs=(pl.BlockSpec(memory_space=pltpu.VMEM), pl.BlockSpec(memory_space=pltpu.VMEM)),
        scratch_shapes=[dataset] * 10
        + [pltpu.VMEM((24, LANES), i32)] * 10
        + [pltpu.SMEM((8, LANES), i32)] * 10
        + [pltpu.VMEM((4, BLOCK, LANES), i32)] * 8
        + [pltpu.VMEM((8, LANES), f32)] * 10
        + [pltpu.VMEM((4, 8, BLOCK), i32)] * 10
        + [pltpu.VMEM((9, 8, LANES), f32),
           pltpu.VMEM((4, 2, BLOCK, LANES), bf16),
           pltpu.VMEM((3, 4, BLOCK, LANES), bf16),
           pltpu.VMEM((3, 2, BLOCK, LANES), bf16),
           pltpu.VMEM((3, 8, LANES), i32),
           pltpu.VMEM((ROWS, 2 * LANES), bf16),
           pltpu.VMEM((BLOCK, LANES), i32),
           pltpu.VMEM((BLOCK, LANES), i32),
           pltpu.VMEM((16, BLOCK, 2 * LANES), f32),
           pltpu.VMEM((2, 4, 4, 4, 48, LANES), f32),
           pltpu.VMEM((4, 4, 4, 48, LANES), f32),
           pltpu.VMEM((2, 4, 48, LANES), f32),
           pltpu.VMEM((2, 4, 48, LANES), f32),
           pltpu.VMEM((4, 4, 48, LANES), f32),
           pltpu.VMEM((4, 4, 48, LANES), f32),
           pltpu.VMEM((4, 4, 48, LANES), f32),
           pltpu.VMEM((4, 48, LANES), f32),
           dma((15,)), dma((15,)), dma((3,)), dma((3,)), dma((12,)), dma((12,)), dma((6,)), dma((4,)),
           dma((9,)), dma((9,)), dma((10,)), dma((9,)), dma((9,)), dma((3, 3)), dma((3, 3)), dma((11,)), dma((11,))],
        compiler_params=pltpu.CompilerParams(collective_id=0, has_side_effects=True, vmem_limit_bytes=60 * 1024 * 1024),
    )(embeddings, labels.reshape(8, LANES), ranking.reshape(8, LANES), send_list, pair_list)


def body(embeddings, labels, ranking, send_list, pair_list):
    scores, centroids = exchange(embeddings, labels, ranking, send_list, pair_list)
    return (scores.reshape(ROWS), centroids)


def solution(mesh):
    return jax.shard_map(
        body,
        mesh=mesh,
        in_specs=(
            P(("group", "dev"), None),
            P(("group", "dev")),
            P(("group", "dev")),
            P(("group", "dev"), None),
            P(("group", "dev"), None),
        ),
        out_specs=(P(("group", "dev")), P(("group", "dev"), None)),
        check_vma=False,
    )
```

```python
import jax
import jax.numpy as jnp
from jax import lax
from jax.experimental import pallas as pl
from jax.experimental.pallas import tpu as pltpu
from jax.sharding import PartitionSpec as P

K = 4096
BLOCK = 256
ROWS = 1024
SLICES = 6
LANES = 128
LOW = -2.0
RANKS = 131072
MESH = pl.DeviceIdType.MESH
M1, M2, M3, X1, X2, P0, P1, P2, P3 = range(9)
PARTS = ((0, 1), (1, 2), (3, 3))


def kernel(emb_in, lab_in, rank_in, send_in, pair_in, scores_out, centroids_out,
           own, m1, m2, m3, x1, x2, p0, p1, p2, p3, *rest):
    metas = rest[0:11]
    lists = rest[11:21]
    cols = rest[21:25]
    accs = rest[25:35]
    flats = rest[35:45]
    own_meta = metas[9]
    (result_in, halves, xa, xp, xmeta, rhs, sums, cores, from_core, in_f, in_b, in2_f, in2_b, in_side, in_x,
     q_send, q_recv, d_send, d_recv, meta_send, meta_recv, list_sem, res_send, res_recv,
     x_send, x_recv, c_send, c_recv, emb, emb_sem) = rest[45:]
    bufs = (m1, m2, m3, x1, x2, p0, p1, p2, p3)
    group = lax.axis_index("group")
    me = lax.axis_index("dev")
    core = lax.rem(me, 2)
    y, z = me // 8, lax.rem(me // 2, 4)
    main = jnp.where(core == 0, z, y)
    side = jnp.where(core == 0, y, z)
    def place(u, w, e):
        return lax.rem(u, 4) * (2 + 6 * e) + lax.rem(w, 4) * (8 - 6 * e) + e

    def at(index):
        return (group, index)

    other = 1 - core
    sources = [place(main + 1, side, core), place(main + 2, side, core), place(main + 3, side, core),
               place(main, side + 3, core), place(main, side + 2, core),
               place(side, main, other), place(side + 1, main, other), place(side + 2, main, other), place(side + 3, main, other)]
    back = at(place(main + 3, side, core))
    forth = at(place(main + 1, side, core))
    along = at(place(main, side + 1, core))
    partner = at(place(side, main, other))

    behind = at(place(main, side + 3, core))
    across = at(place(main, side + 2, core))
    mates = [(lax.rem(group + i, 4), me) for i in (1, 2, 3)]

    barrier = pltpu.get_barrier_semaphore()
    for device in [forth, back, along, behind, partner] + mates:
        pl.semaphore_signal(barrier, inc=1, device_id=device, device_id_type=MESH)

    emb_copy = pltpu.make_async_copy(emb_in, emb, emb_sem.at[0])
    emb_copy.start()
    own_meta[0:8, :] = lab_in[...] * RANKS + rank_in[...]
    own_meta[8:9, 0:32] = send_in[...]
    own_meta[9:10, 0:32] = pair_in[...]

    def normalize(i, carry):
        rows = pl.ds(pl.multiple_of(i * 128, 128), 128)
        values = emb[rows, :].astype(jnp.float32)
        scaled = values * lax.rsqrt(jnp.sum(values * values, axis=-1, keepdims=True) + 1e-06)
        unit = scaled.astype(jnp.bfloat16)
        for c in range(SLICES):
            own[c, i // 2, pl.ds(pl.multiple_of(lax.rem(i, 2) * 128, 128), 128), :] = unit[:, c * LANES:(c + 1) * LANES]
        return carry

    emb_copy.wait()
    lax.fori_loop(0, 8, normalize, 0)
    lane_ids = lax.broadcasted_iota(jnp.int32, (BLOCK, LANES), 1)

    for t in range(2):
        for b in range(2):
            low = own[4 + t, b].astype(jnp.float32)
            high = own[4 + t, b + 2].astype(jnp.float32)
            halves[2 * t, b] = jnp.where(lane_ids < 64, low, pltpu.roll(high, 64, 1)).astype(jnp.bfloat16)
            halves[2 * t + 1, b] = jnp.where(lane_ids < 64, pltpu.roll(low, 64, 1), high).astype(jnp.bfloat16)
    pl.semaphore_wait(barrier, 8)

    started = []

    def remote(src, dst, send, recv, device):
        return pltpu.make_async_remote_copy(src_ref=src, dst_ref=dst, send_sem=send, recv_sem=recv, device_id=device,
                                            device_id_type=MESH)

    def go(copy):
        copy.start()
        started.append(copy)

    legs = {"o": (own, m1, back, 0), "f": (m1, m2, back, 3), "g": (m2, m3, back, 6), "h": (own, m3, forth, 9),
            "x": (own, x1, along, 12), "y": (x1, x2, along, 15)}

    def send(leg, part):
        src, dst, device, sem = legs[leg]
        piece = pl.ds(*PARTS[part])
        go(remote(src.at[piece], dst.at[piece], q_send.at[sem + part], q_recv.at[sem + part], device))

    def arrive(leg, part):
        _, dst, _, sem = legs[leg]
        landed(dst.at[pl.ds(*PARTS[part])], q_recv.at[sem + part])

    def landed(dst, recv):
        remote(dst, dst, res_send.at[0], recv, partner).wait_recv()

    meta_routes = [(9, M1, back), (9, M3, forth), (9, X1, along), (9, 10, behind), (9, P0, partner),
                   (M3, M2, forth), (10, X2, behind), (M1, P1, partner), (M3, P3, partner), (M2, P2, partner)]

    def meta_go(i):
        src, dst, device = meta_routes[i]
        go(remote(metas[src], metas[dst], meta_send.at[i], meta_recv.at[dst], device))

    def mate_copies(i):
        quarter = lax.rem(group + 1 + i, 4)
        go(remote(lab_in, xmeta.at[i], x_send.at[i, 0], x_recv.at[i, 0], mates[i]))
        go(remote(own.at[quarter], xa.at[i], x_send.at[i, 1], x_recv.at[i, 1], mates[i]))
        go(remote(halves.at[quarter], xp.at[i], x_send.at[i, 2], x_recv.at[i, 2], mates[i]))

    for i in range(5):
        meta_go(i)
    send("o", 0)
    send("x", 0)
    mate_copies(0)
    mate_copies(2)
    send("o", 1)
    send("x", 1)
    send("o", 2)
    send("x", 2)
    go(remote(own, p0, d_send.at[0], d_recv.at[0], partner))

    def share(which, first, count, slot):
        src, dst = bufs[which], bufs[which + P1]
        go(remote(src.at[pl.ds(first, count)], dst.at[pl.ds(first, count)], d_send.at[slot], d_recv.at[which + 1], partner))

    def shared_arrival(i):
        dst = (p0, p1, p2, p3)[i]
        remote(dst, dst, d_send.at[0], d_recv.at[i], partner).wait_recv()

    def make_cols(meta, i):
        for r in range(8):
            row = jnp.broadcast_to(meta[r:r + 1, :], (LANES, LANES))
            cols[i][r // 2, (r % 2) * LANES:(r % 2 + 1) * LANES, :] = row.T

    def make_rows(meta, i):
        keys = meta[0:8, :]
        floors = keys & (-RANKS)
        for r in range(8):
            lanes = slice((r % 2) * LANES, (r % 2 + 1) * LANES)
            flats[i][r // 2, 0:1, lanes] = keys[r:r + 1, :]
            flats[i][r // 2, 1:2, lanes] = floors[r:r + 1, :]

    make_cols(own_meta, 0)
    make_rows(own_meta, 9)
    own_list = pltpu.make_async_copy(own_meta.at[pl.ds(8, 8)], lists[9], list_sem.at[9])
    own_list.start()
    for acc in accs:
        acc[...] = jnp.full((8, LANES), LOW, jnp.float32)
    row_ids = lax.broadcasted_iota(jnp.int32, (8, LANES), 0)

    def update(acc, block, row):
        spread = jnp.where(lax.rem(row_ids, 2) == 0, row[:, :LANES], row[:, LANES:])
        acc[...] = jnp.where(row_ids // 2 == block, jnp.maximum(acc[...], spread), acc[...])

    def tile(abuf, acol, aacc, a, bbuf, brows, bacc, b, same=False):
        left = jnp.concatenate([abuf[c, a] for c in range(SLICES)], axis=1)
        right = jnp.concatenate([bbuf[c, b] for c in range(SLICES)], axis=1)
        similar = lax.dot_general(left, right, (((1,), (1,)), ((), ())), preferred_element_type=jnp.float32)
        akey = cols[acol][a]
        afloor = akey & (-RANKS)
        brow = brows[b]
        for_a, for_b = None, []
        for h in range(2):
            lanes = slice(h * LANES, (h + 1) * LANES)
            bkey, bfloor = brow[0:1, lanes], brow[1:2, lanes]
            value = jnp.where(afloor == bfloor, similar[:, lanes], LOW)
            later = bkey < akey
            va = jnp.where(later, value, LOW)
            vb = jnp.where(akey < bkey, value, LOW) if same else jnp.where(later, LOW, value)
            for_a = va if for_a is None else jnp.maximum(for_a, va)
            for_b.append(jnp.max(vb, axis=0, keepdims=True))
        update(aacc, a, jnp.max(for_a.T, axis=0, keepdims=True))
        update(bacc, b, jnp.concatenate(for_b, axis=1))

    def data(i):
        if i is None:
            return own, flats[9], lists[9], accs[9], me
        return bufs[i], flats[i], lists[i], accs[i], sources[i]

    def meet(ai, bi, forward=True, backward=True):
        abuf, _, alist, aacc, adev = data(ai)
        bbuf, brows, blist, bacc, bdev = data(bi)
        col = 0 if ai is None else ai + 1

        if forward:
            tile(abuf, col, aacc, alist[0, bdev], bbuf, brows, bacc, blist[1, adev])
        if backward:
            tile(abuf, col, aacc, alist[1, bdev], bbuf, brows, bacc, blist[0, adev])

    def local(lo, hi):
        def some(i, carry):
            for n in range(5):
                v = i * 5 + n
                k = jnp.where(v >= 4, 1, 0) + jnp.where(v >= 7, 1, 0) + jnp.where(v >= 9, 1, 0)
                l = v - 3 * jnp.where(v >= 4, 1, 0) - 2 * jnp.where(v >= 7, 1, 0) - jnp.where(v >= 9, 1, 0)
                tile(own, 0, accs[9], k, own, flats[9], accs[9], l, same=True)
            return carry

        lax.fori_loop(lo, hi, some, 0)

    def have_meta(i):
        landed(metas[i], meta_recv.at[i])

    def list_copy(i):
        return pltpu.make_async_copy(metas[i].at[pl.ds(8, 8)], lists[i], list_sem.at[i])

    def use_meta(i):
        list_copy(i).start()
        make_rows(metas[i], i)
        if i < 3:
            make_cols(metas[i], i + 1)

    def set_source(points, extra):
        for b in range(4):
            rhs[b * BLOCK:(b + 1) * BLOCK, :LANES] = points[b]
            keep = (lane_ids < 64) if b < 2 else (lane_ids >= 64)
            rhs[b * BLOCK:(b + 1) * BLOCK, LANES:] = jnp.where(keep, extra[b % 2].astype(jnp.float32), 0.0).astype(jnp.bfloat16)

    def add_source(label_ref, lo, hi, mode):
        labels = label_ref[...]
        ys, zs, es = (labels // 256) % 4, (labels // 64) % 4, (labels // 32) % 2
        order = (es * 2048 + jnp.where(es == 0, zs, ys) * 512 + jnp.where(es == 0, ys, zs) * 128 + (labels // 1024) * 32
                 + labels % 32)

        def chunk(i, carry):
            m = lax.rem(i + 2 * other, 4)
            ids = lax.broadcasted_iota(jnp.int32, (ROWS, LANES), 0) + m * ROWS
            hot = jnp.concatenate(
                [jnp.where(order[r:r + 1, :] == ids, 1.0, 0.0).astype(jnp.bfloat16) for r in range(8)], axis=1)
            total = jnp.dot(hot, rhs[...], preferred_element_type=jnp.float32)
            if mode != "first":
                total = total + sums[m]
            if mode != "last":
                sums[m] = total
            else:
                extra = total[:, LANES:]
                extra = extra + pltpu.roll(extra, 64, 1)
                for b in range(32):
                    place_ = (m // 2, 2 * lax.rem(m, 2) + b // 16, (b // 4) % 4, b % 4)
                    cores[(*place_, slice(0, 32))] = total[b * 32:b * 32 + 32, :LANES]
                    cores[(*place_, slice(32, 48))] = jnp.where(
                        lane_ids[:16] < 64, extra[b * 32:b * 32 + 16], extra[b * 32 + 16:b * 32 + 32])
            return carry

        lax.fori_loop(lo, hi, chunk, 0)

    def ring(i):
        return lax.rem(main + i, 4)

    def centroid_send(src, dst, i, device):
        go(remote(src, dst, c_send.at[i], c_recv.at[i], device))

    def finish_centroids():
        quarters = [in_x[lax.rem(group - q + 4, 4)] for q in range(4)]
        tiles = [quarters[q][0:32] for q in range(4)]
        low = lane_ids[:16] < 64
        for t in range(2):
            even, odd = quarters[2 * t][32:48], quarters[2 * t + 1][32:48]
            tiles.append(jnp.concatenate([jnp.where(low, even, pltpu.roll(odd, 64, 1)),
                                          jnp.where(low, pltpu.roll(even, 64, 1), odd)], axis=0))
        squares = tiles[0] * tiles[0]
        for tile_values in tiles[1:]:
            squares = squares + tile_values * tile_values
        scale = lax.rsqrt(jnp.sum(squares, axis=-1, keepdims=True) / 768.0 + 1e-06)
        for c in range(SLICES):
            centroids_out[:, c * LANES:(c + 1) * LANES] = tiles[c] * scale

    def give_back(i):
        go(remote(accs[i], result_in.at[i], res_send.at[i], res_recv.at[i], at(sources[i])))

    def source(i):
        landed(xmeta.at[i], x_recv.at[i, 0])
        landed(xa.at[i], x_recv.at[i, 1])
        landed(xp.at[i], x_recv.at[i, 2])
        set_source(xa.at[i], xp.at[i])

    own_list.wait()
    have_meta(M3)
    meta_go(5)
    have_meta(10)
    meta_go(6)
    have_meta(M1)
    meta_go(7)
    meta_go(8)
    set_source(own.at[group], halves.at[group])
    add_source(lab_in, 0, 4, "first")
    have_meta(M2)
    meta_go(9)
    for i in (X1, X2, P0, P1, P3):
        have_meta(i)
    for i in (M1, M2, M3, X1, X2, P0, P1, P3):
        use_meta(i)
    arrive("o", 0)
    send("f", 0)
    arrive("x", 0)
    send("y", 0)
    send("h", 2)
    mate_copies(1)
    have_meta(P2)
    use_meta(P2)
    local(0, 2)
    source(0)
    add_source(xmeta.at[0], 0, 4, "add")
    source(2)
    add_source(xmeta.at[2], 0, 4, "add")
    arrive("o", 1)
    send("f", 1)
    arrive("f", 0)
    send("g", 0)
    arrive("x", 1)
    send("y", 1)
    for i in range(9):
        list_copy(i).wait()
    source(1)
    add_source(xmeta.at[1], 0, 2, "last")
    centroid_send(cores.at[other], from_core, 0, partner)
    add_source(xmeta.at[1], 2, 4, "last")
    arrive("o", 2)
    send("f", 2)
    share(M1, 0, 6, 1)
    arrive("x", 2)
    send("y", 2)
    shared_arrival(0)
    meet(None, P0, backward=False)
    meet(M1, P0, backward=False)
    meet(None, M1)
    landed(from_core, c_recv.at[0])
    for i in range(4):
        cores[core, i] = cores[core, i] + from_core[i]
    centroid_send(cores.at[core, ring(2), pl.ds(0, 2)], in_f, 1, forth)
    centroid_send(cores.at[core, ring(2), pl.ds(2, 2)], in_b, 2, back)
    meet(None, X1)
    meet(M1, X1)
    arrive("f", 1)
    send("g", 1)
    shared_arrival(1)
    meet(None, P1, backward=False)
    meet(M1, P1, backward=False)
    arrive("y", 0)
    landed(in_f, c_recv.at[1])
    cores[core, ring(1), 0:2] = cores[core, ring(1), 0:2] + in_f[...]
    centroid_send(cores.at[core, ring(1)], in2_f, 3, forth)
    landed(in_b, c_recv.at[2])
    cores[core, ring(3), 2:4] = cores[core, ring(3), 2:4] + in_b[...]
    centroid_send(cores.at[core, ring(3)], in2_b, 4, back)
    arrive("h", 2)
    share(M3, 3, 3, 3)
    arrive("g", 0)
    share(M3, 0, 1, 4)
    arrive("y", 1)
    arrive("f", 2)
    share(M2, 0, 6, 2)
    meet(None, M2, forward=False)
    meet(M2, X1)
    meet(M2, P0, backward=False)
    meet(M2, P1, backward=False)
    landed(in2_f, c_recv.at[3])
    landed(in2_b, c_recv.at[4])
    cores[core, main] = cores[core, main] + in2_f[...] + in2_b[...]
    for i, device in ((1, along), (2, across), (3, behind)):
        centroid_send(cores.at[core, main, lax.rem(side + i, 4)], in_side.at[i], 4 + i, device)
    shared_arrival(2)
    meet(None, P2, backward=False)
    meet(M1, P2, backward=False)
    meet(M2, P2, backward=False)
    arrive("y", 2)
    meet(None, X2, forward=False)
    meet(M1, X2, forward=False)
    meet(M2, X2, forward=False)
    for i in (1, 2, 3):
        landed(in_side.at[i], c_recv.at[4 + i])
    in_side[0] = cores[core, main, side] + in_side[1] + in_side[2] + in_side[3]
    in_x[0] = in_side[0, group]
    for i in (1, 2, 3):
        centroid_send(in_side.at[0, lax.rem(group + i, 4)], in_x.at[i], 7 + i, mates[i - 1])
    arrive("g", 1)
    share(M3, 1, 2, 5)
    for i in (X2, X1):
        meet(M3, i, forward=i == X1)
    for i in (P0, P1, P2):
        meet(M3, i, backward=False)
    for i in (X2, X1, P0, P1, P2):
        give_back(i)
    shared_arrival(3)
    for i in (M3, M2, M1, None):
        meet(i, P3, backward=False)
    for i in (M3, P3, M2, M1):
        give_back(i)

    for i in (1, 2, 3):
        landed(in_x.at[i], c_recv.at[7 + i])
    finish_centroids()
    best = jnp.maximum(accs[9][...], 0.0)
    for i in range(9):
        remote(result_in.at[i], result_in.at[i], res_send.at[i], res_recv.at[i], partner).wait_recv()
        best = jnp.maximum(best, result_in[i])
    scores_out[...] = best
    for copy in started:
        copy.wait_send()


def exchange(embeddings, labels, ranking, send_list, pair_list):
    dataset = pltpu.VMEM((SLICES, 4, BLOCK, LANES), jnp.bfloat16)
    dma = pltpu.SemaphoreType.DMA
    f32, bf16, i32 = jnp.float32, jnp.bfloat16, jnp.int32
    return pl.pallas_call(
        kernel,
        out_shape=(jax.ShapeDtypeStruct((8, LANES), f32), jax.ShapeDtypeStruct((32, SLICES * LANES), f32)),
        in_specs=[pl.BlockSpec(memory_space=pl.ANY)] + [pl.BlockSpec(memory_space=pltpu.VMEM)] * 4,
        out_specs=(pl.BlockSpec(memory_space=pltpu.VMEM), pl.BlockSpec(memory_space=pltpu.VMEM)),
        scratch_shapes=[dataset] * 10
        + [pltpu.VMEM((16, LANES), i32)] * 11
        + [pltpu.SMEM((8, LANES), i32)] * 10
        + [pltpu.VMEM((4, BLOCK, LANES), i32)] * 4
        + [pltpu.VMEM((8, LANES), f32)] * 10
        + [pltpu.VMEM((4, 8, BLOCK), i32)] * 10
        + [pltpu.VMEM((9, 8, LANES), f32),
           pltpu.VMEM((4, 2, BLOCK, LANES), bf16),
           pltpu.VMEM((3, 4, BLOCK, LANES), bf16),
           pltpu.VMEM((3, 2, BLOCK, LANES), bf16),
           pltpu.VMEM((3, 8, LANES), i32),
           pltpu.VMEM((ROWS, 2 * LANES), bf16),
           pltpu.VMEM((4, ROWS, 2 * LANES), f32),
           pltpu.VMEM((2, 4, 4, 4, 48, LANES), f32),
           pltpu.VMEM((4, 4, 4, 48, LANES), f32),
           pltpu.VMEM((2, 4, 48, LANES), f32),
           pltpu.VMEM((2, 4, 48, LANES), f32),
           pltpu.VMEM((4, 4, 48, LANES), f32),
           pltpu.VMEM((4, 4, 48, LANES), f32),
           pltpu.VMEM((4, 4, 48, LANES), f32),
           pltpu.VMEM((4, 48, LANES), f32),
           dma((18,)), dma((18,)), dma((6,)), dma((4,)),
           dma((10,)), dma((11,)), dma((10,)), dma((9,)), dma((9,)), dma((3, 3)), dma((3, 3)), dma((11,)), dma((11,)),
           pltpu.VMEM((ROWS, SLICES * LANES), bf16), dma((1,))],
        compiler_params=pltpu.CompilerParams(collective_id=0, has_side_effects=True, vmem_limit_bytes=60 * 1024 * 1024),
    )(embeddings, labels.reshape(8, LANES), ranking.reshape(8, LANES), send_list, pair_list)


def body(embeddings, labels, ranking, send_list, pair_list):
    scores, centroids = exchange(embeddings, labels, ranking, send_list, pair_list)
    return (scores.reshape(ROWS), centroids)


def solution(mesh):
    return jax.shard_map(
        body,
        mesh=mesh,
        in_specs=(
            P(("group", "dev"), None),
            P(("group", "dev")),
            P(("group", "dev")),
            P(("group", "dev"), None),
            P(("group", "dev"), None),
        ),
        out_specs=(P(("group", "dev")), P(("group", "dev"), None)),
        check_vma=False,
    )
```

```python
import jax
import jax.numpy as jnp
from jax import lax
from jax.experimental import pallas as pl
from jax.experimental.pallas import tpu as pltpu
from jax.sharding import PartitionSpec as P

K = 4096
BLOCK = 256
ROWS = 1024
SLICES = 6
LANES = 128
LOW = -2.0
RANKS = 131072
MESH = pl.DeviceIdType.MESH
M1, M2, M3, X1, X2, P0, P1, P2, P3 = range(9)
PARTS = ((0, 1), (1, 2), (3, 3))


def kernel(emb_in, lab_in, rank_in, send_in, pair_in, scores_out, centroids_out,
           own, m1, m2, m3, x1, x2, p0, p1, p2, p3, *rest):
    metas = rest[0:11]
    lists = rest[11:21]
    cols = rest[21:25]
    accs = rest[25:35]
    flats = rest[35:45]
    own_meta = metas[9]
    (result_in, halves, xa, xp, xmeta, rhs, sums, cores, from_core, in_f, in_b, in2_f, in2_b, in_side, in_x,
     q_send, q_recv, d_send, d_recv, meta_send, meta_recv, list_sem, res_send, res_recv,
     x_send, x_recv, c_send, c_recv, emb, emb_sem) = rest[45:]
    bufs = (m1, m2, m3, x1, x2, p0, p1, p2, p3)
    group = lax.axis_index("group")
    me = lax.axis_index("dev")
    core = lax.rem(me, 2)
    y, z = me // 8, lax.rem(me // 2, 4)
    main = jnp.where(core == 0, z, y)
    side = jnp.where(core == 0, y, z)
    def place(u, w, e):
        return lax.rem(u, 4) * (2 + 6 * e) + lax.rem(w, 4) * (8 - 6 * e) + e

    def at(index):
        return (group, index)

    other = 1 - core
    sources = [place(main + 1, side, core), place(main + 2, side, core), place(main + 3, side, core),
               place(main, side + 3, core), place(main, side + 2, core),
               place(side, main, other), place(side + 1, main, other), place(side + 2, main, other), place(side + 3, main, other)]
    back = at(place(main + 3, side, core))
    forth = at(place(main + 1, side, core))
    along = at(place(main, side + 1, core))
    partner = at(place(side, main, other))

    behind = at(place(main, side + 3, core))
    across = at(place(main, side + 2, core))
    mates = [(lax.rem(group + i, 4), me) for i in (1, 2, 3)]

    barrier = pltpu.get_barrier_semaphore()
    for device in [forth, back, along, behind, partner] + mates:
        pl.semaphore_signal(barrier, inc=1, device_id=device, device_id_type=MESH)

    emb_copy = pltpu.make_async_copy(emb_in, emb, emb_sem.at[0])
    emb_copy.start()
    own_meta[0:8, :] = lab_in[...] * RANKS + rank_in[...]
    own_meta[8:9, 0:32] = send_in[...]
    own_meta[9:10, 0:32] = pair_in[...]

    def normalize(i, carry):
        rows = pl.ds(pl.multiple_of(i * 128, 128), 128)
        values = emb[rows, :].astype(jnp.float32)
        scaled = values * lax.rsqrt(jnp.sum(values * values, axis=-1, keepdims=True) + 1e-06)
        unit = scaled.astype(jnp.bfloat16)
        for c in range(SLICES):
            own[c, i // 2, pl.ds(pl.multiple_of(lax.rem(i, 2) * 128, 128), 128), :] = unit[:, c * LANES:(c + 1) * LANES]
        return carry

    emb_copy.wait()
    lax.fori_loop(0, 8, normalize, 0)
    lane_ids = lax.broadcasted_iota(jnp.int32, (BLOCK, LANES), 1)

    for t in range(2):
        for b in range(2):
            low = own[4 + t, b].astype(jnp.float32)
            high = own[4 + t, b + 2].astype(jnp.float32)
            halves[2 * t, b] = jnp.where(lane_ids < 64, low, pltpu.roll(high, 64, 1)).astype(jnp.bfloat16)
            halves[2 * t + 1, b] = jnp.where(lane_ids < 64, pltpu.roll(low, 64, 1), high).astype(jnp.bfloat16)
    pl.semaphore_wait(barrier, 8)

    started = []

    def remote(src, dst, send, recv, device):
        return pltpu.make_async_remote_copy(src_ref=src, dst_ref=dst, send_sem=send, recv_sem=recv, device_id=device,
                                            device_id_type=MESH)

    def go(copy):
        copy.start()
        started.append(copy)

    legs = {"o": (own, m1, back, 0), "f": (m1, m2, back, 3), "g": (m2, m3, back, 6), "h": (own, m3, forth, 9),
            "x": (own, x1, along, 12), "y": (x1, x2, along, 15)}

    def send(leg, part):
        src, dst, device, sem = legs[leg]
        piece = pl.ds(*PARTS[part])
        go(remote(src.at[piece], dst.at[piece], q_send.at[sem + part], q_recv.at[sem + part], device))

    def arrive(leg, part):
        _, dst, _, sem = legs[leg]
        landed(dst.at[pl.ds(*PARTS[part])], q_recv.at[sem + part])

    def landed(dst, recv):
        remote(dst, dst, res_send.at[0], recv, partner).wait_recv()

    meta_routes = [(9, M1, back), (9, M3, forth), (9, X1, along), (9, 10, behind), (9, P0, partner),
                   (M3, M2, forth), (10, X2, behind), (M1, P1, partner), (M3, P3, partner), (M2, P2, partner)]

    def meta_go(i):
        src, dst, device = meta_routes[i]
        go(remote(metas[src], metas[dst], meta_send.at[i], meta_recv.at[dst], device))

    def mate_copies(i):
        quarter = lax.rem(group + 1 + i, 4)
        go(remote(lab_in, xmeta.at[i], x_send.at[i, 0], x_recv.at[i, 0], mates[i]))
        go(remote(own.at[quarter], xa.at[i], x_send.at[i, 1], x_recv.at[i, 1], mates[i]))
        go(remote(halves.at[quarter], xp.at[i], x_send.at[i, 2], x_recv.at[i, 2], mates[i]))

    for i in range(5):
        meta_go(i)
    send("o", 0)
    send("x", 0)
    mate_copies(0)
    mate_copies(2)
    send("o", 1)
    send("x", 1)
    send("o", 2)
    send("x", 2)
    go(remote(own, p0, d_send.at[0], d_recv.at[0], partner))

    def share(which, first, count, slot):
        src, dst = bufs[which], bufs[which + P1]
        go(remote(src.at[pl.ds(first, count)], dst.at[pl.ds(first, count)], d_send.at[slot], d_recv.at[which + 1], partner))

    def shared_arrival(i):
        dst = (p0, p1, p2, p3)[i]
        remote(dst, dst, d_send.at[0], d_recv.at[i], partner).wait_recv()

    def make_cols(meta, i):
        for r in range(8):
            row = jnp.broadcast_to(meta[r:r + 1, :], (LANES, LANES))
            cols[i][r // 2, (r % 2) * LANES:(r % 2 + 1) * LANES, :] = row.T

    def make_rows(meta, i):
        keys = meta[0:8, :]
        floors = keys & (-RANKS)
        for r in range(8):
            lanes = slice((r % 2) * LANES, (r % 2 + 1) * LANES)
            flats[i][r // 2, 0:1, lanes] = keys[r:r + 1, :]
            flats[i][r // 2, 1:2, lanes] = floors[r:r + 1, :]

    make_cols(own_meta, 0)
    make_rows(own_meta, 9)
    own_list = pltpu.make_async_copy(own_meta.at[pl.ds(8, 8)], lists[9], list_sem.at[9])
    own_list.start()
    for acc in accs:
        acc[...] = jnp.full((8, LANES), LOW, jnp.float32)
    row_ids = lax.broadcasted_iota(jnp.int32, (8, LANES), 0)

    def update(acc, block, row):
        spread = jnp.where(lax.rem(row_ids, 2) == 0, row[:, :LANES], row[:, LANES:])
        acc[...] = jnp.where(row_ids // 2 == block, jnp.maximum(acc[...], spread), acc[...])

    def tile(abuf, acol, aacc, a, bbuf, brows, bacc, b, same=False):
        left = jnp.concatenate([abuf[c, a] for c in range(SLICES)], axis=1)
        right = jnp.concatenate([bbuf[c, b] for c in range(SLICES)], axis=1)
        similar = lax.dot_general(left, right, (((1,), (1,)), ((), ())), preferred_element_type=jnp.float32)
        akey = cols[acol][a]
        afloor = akey & (-RANKS)
        brow = brows[b]
        for_a, for_b = None, []
        for h in range(2):
            lanes = slice(h * LANES, (h + 1) * LANES)
            bkey, bfloor = brow[0:1, lanes], brow[1:2, lanes]
            value = jnp.where(afloor == bfloor, similar[:, lanes], LOW)
            later = bkey < akey
            va = jnp.where(later, value, LOW)
            vb = jnp.where(akey < bkey, value, LOW) if same else jnp.where(later, LOW, value)
            for_a = va if for_a is None else jnp.maximum(for_a, va)
            for_b.append(jnp.max(vb, axis=0, keepdims=True))
        update(aacc, a, jnp.max(for_a.T, axis=0, keepdims=True))
        update(bacc, b, jnp.concatenate(for_b, axis=1))

    def data(i):
        if i is None:
            return own, flats[9], lists[9], accs[9], me
        return bufs[i], flats[i], lists[i], accs[i], sources[i]

    def meet(ai, bi, forward=True, backward=True):
        abuf, _, alist, aacc, adev = data(ai)
        bbuf, brows, blist, bacc, bdev = data(bi)
        col = 0 if ai is None else ai + 1

        if forward:
            tile(abuf, col, aacc, alist[0, bdev], bbuf, brows, bacc, blist[1, adev])
        if backward:
            tile(abuf, col, aacc, alist[1, bdev], bbuf, brows, bacc, blist[0, adev])

    def local(lo, hi):
        def some(i, carry):
            for n in range(5):
                v = i * 5 + n
                k = jnp.where(v >= 4, 1, 0) + jnp.where(v >= 7, 1, 0) + jnp.where(v >= 9, 1, 0)
                l = v - 3 * jnp.where(v >= 4, 1, 0) - 2 * jnp.where(v >= 7, 1, 0) - jnp.where(v >= 9, 1, 0)
                tile(own, 0, accs[9], k, own, flats[9], accs[9], l, same=True)
            return carry

        lax.fori_loop(lo, hi, some, 0)

    def have_meta(i):
        landed(metas[i], meta_recv.at[i])

    def list_copy(i):
        return pltpu.make_async_copy(metas[i].at[pl.ds(8, 8)], lists[i], list_sem.at[i])

    def use_meta(i):
        list_copy(i).start()
        make_rows(metas[i], i)
        if i < 3:
            make_cols(metas[i], i + 1)

    def set_source(points, extra):
        for b in range(4):
            rhs[b * BLOCK:(b + 1) * BLOCK, :LANES] = points[b]
            keep = (lane_ids < 64) if b < 2 else (lane_ids >= 64)
            rhs[b * BLOCK:(b + 1) * BLOCK, LANES:] = jnp.where(keep, extra[b % 2].astype(jnp.float32), 0.0).astype(jnp.bfloat16)

    def add_source(label_ref, lo, hi, mode):
        labels = label_ref[...]
        ys, zs, es = (labels // 256) % 4, (labels // 64) % 4, (labels // 32) % 2
        order = (es * 2048 + jnp.where(es == 0, zs, ys) * 512 + jnp.where(es == 0, ys, zs) * 128 + (labels // 1024) * 32
                 + labels % 32)

        def chunk(i, carry):
            m = lax.rem(i + 2 * other, 4)
            ids = lax.broadcasted_iota(jnp.int32, (ROWS, LANES), 0) + m * ROWS
            hot = jnp.concatenate(
                [jnp.where(order[r:r + 1, :] == ids, 1.0, 0.0).astype(jnp.bfloat16) for r in range(8)], axis=1)
            total = jnp.dot(hot, rhs[...], preferred_element_type=jnp.float32)
            if mode != "first":
                total = total + sums[m]
            if mode != "last":
                sums[m] = total
            else:
                extra = total[:, LANES:]
                extra = extra + pltpu.roll(extra, 64, 1)
                for b in range(32):
                    place_ = (m // 2, 2 * lax.rem(m, 2) + b // 16, (b // 4) % 4, b % 4)
                    cores[(*place_, slice(0, 32))] = total[b * 32:b * 32 + 32, :LANES]
                    cores[(*place_, slice(32, 48))] = jnp.where(
                        lane_ids[:16] < 64, extra[b * 32:b * 32 + 16], extra[b * 32 + 16:b * 32 + 32])
            return carry

        lax.fori_loop(lo, hi, chunk, 0)

    def ring(i):
        return lax.rem(main + i, 4)

    def centroid_send(src, dst, i, device):
        go(remote(src, dst, c_send.at[i], c_recv.at[i], device))

    def finish_centroids():
        quarters = [in_x[lax.rem(group - q + 4, 4)] for q in range(4)]
        tiles = [quarters[q][0:32] for q in range(4)]
        low = lane_ids[:16] < 64
        for t in range(2):
            even, odd = quarters[2 * t][32:48], quarters[2 * t + 1][32:48]
            tiles.append(jnp.concatenate([jnp.where(low, even, pltpu.roll(odd, 64, 1)),
                                          jnp.where(low, pltpu.roll(even, 64, 1), odd)], axis=0))
        squares = tiles[0] * tiles[0]
        for tile_values in tiles[1:]:
            squares = squares + tile_values * tile_values
        scale = lax.rsqrt(jnp.sum(squares, axis=-1, keepdims=True) / 768.0 + 1e-06)
        for c in range(SLICES):
            centroids_out[:, c * LANES:(c + 1) * LANES] = tiles[c] * scale

    def give_back(i):
        go(remote(accs[i], result_in.at[i], res_send.at[i], res_recv.at[i], at(sources[i])))

    def source(i):
        landed(xmeta.at[i], x_recv.at[i, 0])
        landed(xa.at[i], x_recv.at[i, 1])
        landed(xp.at[i], x_recv.at[i, 2])
        set_source(xa.at[i], xp.at[i])

    own_list.wait()
    have_meta(M3)
    meta_go(5)
    have_meta(10)
    meta_go(6)
    have_meta(M1)
    meta_go(7)
    meta_go(8)
    set_source(own.at[group], halves.at[group])
    add_source(lab_in, 0, 4, "first")
    have_meta(M2)
    meta_go(9)
    for i in (X1, X2, P0, P1, P3):
        have_meta(i)
    for i in (M1, M2, M3, X1, X2, P0, P1, P3):
        use_meta(i)
    arrive("o", 0)
    send("f", 0)
    arrive("x", 0)
    send("y", 0)
    mate_copies(1)
    send("h", 2)
    have_meta(P2)
    use_meta(P2)
    local(0, 2)
    source(0)
    add_source(xmeta.at[0], 0, 4, "add")
    arrive("o", 1)
    send("f", 1)
    arrive("x", 1)
    send("y", 1)
    source(2)
    add_source(xmeta.at[2], 0, 4, "add")
    arrive("o", 2)
    send("f", 2)
    share(M1, 0, 6, 1)
    source(1)
    add_source(xmeta.at[1], 0, 2, "last")
    centroid_send(cores.at[other], from_core, 0, partner)
    add_source(xmeta.at[1], 2, 4, "last")
    landed(from_core, c_recv.at[0])
    for i in range(4):
        cores[core, i] = cores[core, i] + from_core[i]
    centroid_send(cores.at[core, ring(2), pl.ds(0, 2)], in_f, 1, forth)
    centroid_send(cores.at[core, ring(2), pl.ds(2, 2)], in_b, 2, back)
    for i in range(9):
        list_copy(i).wait()
    shared_arrival(0)
    meet(None, P0, backward=False)
    meet(M1, P0, backward=False)
    meet(None, M1)
    arrive("x", 2)
    send("y", 2)
    arrive("f", 0)
    send("g", 0)
    meet(None, X1)
    meet(M1, X1)
    arrive("f", 1)
    send("g", 1)
    landed(in_b, c_recv.at[2])
    cores[core, ring(3), 2:4] = cores[core, ring(3), 2:4] + in_b[...]
    centroid_send(cores.at[core, ring(3)], in2_b, 4, back)
    arrive("y", 0)
    landed(in_f, c_recv.at[1])
    cores[core, ring(1), 0:2] = cores[core, ring(1), 0:2] + in_f[...]
    centroid_send(cores.at[core, ring(1)], in2_f, 3, forth)
    shared_arrival(1)
    meet(None, P1, backward=False)
    meet(M1, P1, backward=False)
    arrive("f", 2)
    share(M2, 0, 6, 2)
    meet(None, M2, forward=False)
    meet(M2, X1)
    meet(M2, P0, backward=False)
    meet(M2, P1, backward=False)
    arrive("g", 0)
    share(M3, 0, 1, 4)
    arrive("y", 1)
    arrive("h", 2)
    share(M3, 3, 3, 3)
    shared_arrival(2)
    meet(None, P2, backward=False)
    meet(M1, P2, backward=False)
    meet(M2, P2, backward=False)
    arrive("g", 1)
    share(M3, 1, 2, 5)
    landed(in2_f, c_recv.at[3])
    landed(in2_b, c_recv.at[4])
    cores[core, main] = cores[core, main] + in2_f[...] + in2_b[...]
    for i, device in ((1, along), (2, across), (3, behind)):
        centroid_send(cores.at[core, main, lax.rem(side + i, 4)], in_side.at[i], 4 + i, device)
    arrive("y", 2)
    for i in (None, M1, M2, M3):
        meet(i, X2, forward=False)
    meet(M3, X1)
    for i in (P0, P1, P2):
        meet(M3, i, backward=False)
    for i in (X2, X1, P0, P1, P2):
        give_back(i)
    shared_arrival(3)
    for i in (M3, M2, M1, None):
        meet(i, P3, backward=False)
    for i in (M3, P3, M2, M1):
        give_back(i)
    for i in (1, 2, 3):
        landed(in_side.at[i], c_recv.at[4 + i])
    in_side[0] = cores[core, main, side] + in_side[1] + in_side[2] + in_side[3]
    in_x[0] = in_side[0, group]
    for i in (1, 2, 3):
        centroid_send(in_side.at[0, lax.rem(group + i, 4)], in_x.at[i], 7 + i, mates[i - 1])
    for i in (1, 2, 3):
        landed(in_x.at[i], c_recv.at[7 + i])
    finish_centroids()
    best = jnp.maximum(accs[9][...], 0.0)
    for i in range(9):
        remote(result_in.at[i], result_in.at[i], res_send.at[i], res_recv.at[i], partner).wait_recv()
        best = jnp.maximum(best, result_in[i])
    scores_out[...] = best
    for copy in started:
        copy.wait_send()


def exchange(embeddings, labels, ranking, send_list, pair_list):
    dataset = pltpu.VMEM((SLICES, 4, BLOCK, LANES), jnp.bfloat16)
    dma = pltpu.SemaphoreType.DMA
    f32, bf16, i32 = jnp.float32, jnp.bfloat16, jnp.int32
    return pl.pallas_call(
        kernel,
        out_shape=(jax.ShapeDtypeStruct((8, LANES), f32), jax.ShapeDtypeStruct((32, SLICES * LANES), f32)),
        in_specs=[pl.BlockSpec(memory_space=pl.ANY)] + [pl.BlockSpec(memory_space=pltpu.VMEM)] * 4,
        out_specs=(pl.BlockSpec(memory_space=pltpu.VMEM), pl.BlockSpec(memory_space=pltpu.VMEM)),
        scratch_shapes=[dataset] * 10
        + [pltpu.VMEM((16, LANES), i32)] * 11
        + [pltpu.SMEM((8, LANES), i32)] * 10
        + [pltpu.VMEM((4, BLOCK, LANES), i32)] * 4
        + [pltpu.VMEM((8, LANES), f32)] * 10
        + [pltpu.VMEM((4, 8, BLOCK), i32)] * 10
        + [pltpu.VMEM((9, 8, LANES), f32),
           pltpu.VMEM((4, 2, BLOCK, LANES), bf16),
           pltpu.VMEM((3, 4, BLOCK, LANES), bf16),
           pltpu.VMEM((3, 2, BLOCK, LANES), bf16),
           pltpu.VMEM((3, 8, LANES), i32),
           pltpu.VMEM((ROWS, 2 * LANES), bf16),
           pltpu.VMEM((4, ROWS, 2 * LANES), f32),
           pltpu.VMEM((2, 4, 4, 4, 48, LANES), f32),
           pltpu.VMEM((4, 4, 4, 48, LANES), f32),
           pltpu.VMEM((2, 4, 48, LANES), f32),
           pltpu.VMEM((2, 4, 48, LANES), f32),
           pltpu.VMEM((4, 4, 48, LANES), f32),
           pltpu.VMEM((4, 4, 48, LANES), f32),
           pltpu.VMEM((4, 4, 48, LANES), f32),
           pltpu.VMEM((4, 48, LANES), f32),
           dma((18,)), dma((18,)), dma((6,)), dma((4,)),
           dma((10,)), dma((11,)), dma((10,)), dma((9,)), dma((9,)), dma((3, 3)), dma((3, 3)), dma((11,)), dma((11,)),
           pltpu.VMEM((ROWS, SLICES * LANES), bf16), dma((1,))],
        compiler_params=pltpu.CompilerParams(collective_id=0, has_side_effects=True, vmem_limit_bytes=60 * 1024 * 1024),
    )(embeddings, labels.reshape(8, LANES), ranking.reshape(8, LANES), send_list, pair_list)


def store_kernel(scores_in, centroids_in, scores_out, centroids_out):
    scores_out[...] = jnp.maximum(scores_in[...], 0.0)
    centroids_out[...] = centroids_in[...]


def store(scores, centroids):
    return pl.pallas_call(
        store_kernel,
        out_shape=(jax.ShapeDtypeStruct(scores.shape, scores.dtype), jax.ShapeDtypeStruct(centroids.shape, centroids.dtype)),
        in_specs=[pl.BlockSpec(memory_space=pltpu.VMEM)] * 2,
        out_specs=(pl.BlockSpec(memory_space=pltpu.VMEM), pl.BlockSpec(memory_space=pltpu.VMEM)),
    )(scores, centroids)


def body(embeddings, labels, ranking, send_list, pair_list):
    scores, centroids = exchange(embeddings, labels, ranking, send_list, pair_list)
    scores, centroids = store(scores, centroids)
    return (scores.reshape(ROWS), centroids)


def solution(mesh):
    return jax.shard_map(
        body,
        mesh=mesh,
        in_specs=(
            P(("group", "dev"), None),
            P(("group", "dev")),
            P(("group", "dev")),
            P(("group", "dev"), None),
            P(("group", "dev"), None),
        ),
        out_specs=(P(("group", "dev")), P(("group", "dev"), None)),
        check_vma=False,
    )
```

```python
import jax
import jax.numpy as jnp
from jax import lax
from jax.experimental import pallas as pl
from jax.experimental.pallas import tpu as pltpu
from jax.sharding import PartitionSpec as P

K = 4096
BLOCK = 256
ROWS = 1024
SLICES = 6
LANES = 128
LOW = -2.0
RANKS = 131072
MESH = pl.DeviceIdType.MESH
M1, M2, M3, X1, X2, P0, P1, P2, P3 = range(9)
PARTS = ((0, 1), (1, 2), (3, 3))


def kernel(emb_hbm, lab_hbm, rank_hbm, send_hbm, pair_hbm, scores_out, centroids_out,
           own, m1, m2, m3, x1, x2, p0, p1, p2, p3, *rest):
    metas = rest[0:11]
    lists = rest[11:21]
    cols = rest[21:25]
    accs = rest[25:35]
    flats = rest[35:45]
    own_meta = metas[9]
    (result_in, halves, xa, xp, xmeta, rhs, sums, cores, from_core, in_f, in_b, in2_f, in2_b, in_last,
     q_send, q_recv, d_send, d_recv, meta_send, meta_recv, list_sem, res_send, res_recv,
     x_send, x_recv, c_send, c_recv, emb, lab_in, rank_in, send_in, pair_in, in_sem) = rest[45:]
    bufs = (m1, m2, m3, x1, x2, p0, p1, p2, p3)
    loads = [pltpu.make_async_copy(src, dst, in_sem.at[i]) for i, (src, dst) in enumerate(
        ((emb_hbm, emb), (lab_hbm, lab_in), (rank_hbm, rank_in), (send_hbm, send_in), (pair_hbm, pair_in)))]
    for copy in loads:
        copy.start()
    group = lax.axis_index("group")
    me = lax.axis_index("dev")
    core = lax.rem(me, 2)
    y, z = me // 8, lax.rem(me // 2, 4)
    main = jnp.where(core == 0, z, y)
    side = jnp.where(core == 0, y, z)
    def place(u, w, e):
        return lax.rem(u, 4) * (2 + 6 * e) + lax.rem(w, 4) * (8 - 6 * e) + e

    def at(index):
        return (group, index)

    other = 1 - core
    sources = [place(main + 1, side, core), place(main + 2, side, core), place(main + 3, side, core),
               place(main, side + 3, core), place(main, side + 2, core),
               place(side, main, other), place(side + 1, main, other), place(side + 2, main, other), place(side + 3, main, other)]
    back = at(place(main + 3, side, core))
    forth = at(place(main + 1, side, core))
    along = at(place(main, side + 1, core))
    partner = at(place(side, main, other))

    behind = at(place(main, side + 3, core))
    mates = [(lax.rem(group + i, 4), me) for i in (1, 2, 3)]

    barrier = pltpu.get_barrier_semaphore()
    for device in [forth, back, along, behind, partner] + mates:
        pl.semaphore_signal(barrier, inc=1, device_id=device, device_id_type=MESH)

    for copy in loads[1:]:
        copy.wait()
    own_meta[0:8, :] = lab_in[...] * RANKS + rank_in[...]
    own_meta[8:9, 0:32] = send_in[...]
    own_meta[9:10, 0:32] = pair_in[...]

    def normalize(i, carry):
        rows = pl.ds(pl.multiple_of(i * 128, 128), 128)
        values = emb[rows, :].astype(jnp.float32)
        scaled = values * lax.rsqrt(jnp.sum(values * values, axis=-1, keepdims=True) + 1e-06)
        unit = scaled.astype(jnp.bfloat16)
        for c in range(SLICES):
            own[c, i // 2, pl.ds(pl.multiple_of(lax.rem(i, 2) * 128, 128), 128), :] = unit[:, c * LANES:(c + 1) * LANES]
        return carry

    loads[0].wait()
    lax.fori_loop(0, 8, normalize, 0)
    lane_ids = lax.broadcasted_iota(jnp.int32, (BLOCK, LANES), 1)

    for t in range(2):
        for b in range(2):
            low = own[4 + t, b].astype(jnp.float32)
            high = own[4 + t, b + 2].astype(jnp.float32)
            halves[2 * t, b] = jnp.where(lane_ids < 64, low, pltpu.roll(high, 64, 1)).astype(jnp.bfloat16)
            halves[2 * t + 1, b] = jnp.where(lane_ids < 64, pltpu.roll(low, 64, 1), high).astype(jnp.bfloat16)
    pl.semaphore_wait(barrier, 8)

    started = []

    def remote(src, dst, send, recv, device):
        return pltpu.make_async_remote_copy(src_ref=src, dst_ref=dst, send_sem=send, recv_sem=recv, device_id=device,
                                            device_id_type=MESH)

    def go(copy):
        copy.start()
        started.append(copy)

    def drain(count):
        for copy in started[:count]:
            copy.wait_send()
        del started[:count]

    legs = {"o": (own, m1, back, 0), "f": (m1, m2, back, 3), "g": (m2, m3, back, 6), "h": (own, m3, forth, 9),
            "x": (own, x1, along, 12), "y": (x1, x2, along, 15)}

    def send(leg, part):
        src, dst, device, sem = legs[leg]
        piece = pl.ds(*PARTS[part])
        go(remote(src.at[piece], dst.at[piece], q_send.at[sem + part], q_recv.at[sem + part], device))

    def arrive(leg, part):
        _, dst, _, sem = legs[leg]
        landed(dst.at[pl.ds(*PARTS[part])], q_recv.at[sem + part])

    def landed(dst, recv):
        remote(dst, dst, res_send.at[0], recv, partner).wait_recv()

    meta_routes = [(9, M1, back), (9, M3, forth), (9, X1, along), (9, 10, behind), (9, P0, partner),
                   (M3, M2, forth), (10, X2, behind), (M1, P1, partner), (M3, P3, partner), (M2, P2, partner)]

    def meta_go(i):
        src, dst, device = meta_routes[i]
        go(remote(metas[src], metas[dst], meta_send.at[i], meta_recv.at[dst], device))

    def mate_copies(i):
        quarter = lax.rem(group + 1 + i, 4)
        go(remote(lab_in, xmeta.at[i], x_send.at[i, 0], x_recv.at[i, 0], mates[i]))
        go(remote(own.at[quarter], xa.at[i], x_send.at[i, 1], x_recv.at[i, 1], mates[i]))
        go(remote(halves.at[quarter], xp.at[i], x_send.at[i, 2], x_recv.at[i, 2], mates[i]))

    for i in range(5):
        meta_go(i)
    send("o", 0)
    send("x", 0)
    mate_copies(0)
    mate_copies(2)
    send("o", 1)
    send("x", 1)
    send("o", 2)
    send("x", 2)
    go(remote(own, p0, d_send.at[0], d_recv.at[0], partner))

    def share(which, first, count, slot):
        src, dst = bufs[which], bufs[which + P1]
        go(remote(src.at[pl.ds(first, count)], dst.at[pl.ds(first, count)], d_send.at[slot], d_recv.at[which + 1], partner))

    def shared_arrival(i):
        dst = (p0, p1, p2, p3)[i]
        remote(dst, dst, d_send.at[0], d_recv.at[i], partner).wait_recv()

    def make_cols(meta, i):
        for r in range(8):
            row = jnp.broadcast_to(meta[r:r + 1, :], (LANES, LANES))
            cols[i][r // 2, (r % 2) * LANES:(r % 2 + 1) * LANES, :] = row.T

    def make_rows(meta, i):
        keys = meta[0:8, :]
        floors = keys & (-RANKS)
        for r in range(8):
            lanes = slice((r % 2) * LANES, (r % 2 + 1) * LANES)
            flats[i][r // 2, 0:1, lanes] = keys[r:r + 1, :]
            flats[i][r // 2, 1:2, lanes] = floors[r:r + 1, :]

    make_cols(own_meta, 0)
    make_rows(own_meta, 9)
    own_list = pltpu.make_async_copy(own_meta.at[pl.ds(8, 8)], lists[9], list_sem.at[9])
    own_list.start()
    for acc in accs:
        acc[...] = jnp.full((8, LANES), LOW, jnp.float32)
    row_ids = lax.broadcasted_iota(jnp.int32, (8, LANES), 0)

    def update(acc, block, row):
        spread = jnp.where(lax.rem(row_ids, 2) == 0, row[:, :LANES], row[:, LANES:])
        acc[...] = jnp.where(row_ids // 2 == block, jnp.maximum(acc[...], spread), acc[...])

    def tile(abuf, acol, aacc, a, bbuf, brows, bacc, b, same=False):
        left = jnp.concatenate([abuf[c, a] for c in range(SLICES)], axis=1)
        right = jnp.concatenate([bbuf[c, b] for c in range(SLICES)], axis=1)
        similar = lax.dot_general(left, right, (((1,), (1,)), ((), ())), preferred_element_type=jnp.float32)
        akey = cols[acol][a]
        afloor = akey & (-RANKS)
        brow = brows[b]
        for_a, for_b = None, []
        for h in range(2):
            lanes = slice(h * LANES, (h + 1) * LANES)
            bkey, bfloor = brow[0:1, lanes], brow[1:2, lanes]
            value = jnp.where(afloor == bfloor, similar[:, lanes], LOW)
            later = bkey < akey
            va = jnp.where(later, value, LOW)
            vb = jnp.where(akey < bkey, value, LOW) if same else jnp.where(later, LOW, value)
            for_a = va if for_a is None else jnp.maximum(for_a, va)
            for_b.append(jnp.max(vb, axis=0, keepdims=True))
        update(aacc, a, jnp.max(for_a.T, axis=0, keepdims=True))
        update(bacc, b, jnp.concatenate(for_b, axis=1))

    def data(i):
        if i is None:
            return own, flats[9], lists[9], accs[9], me
        return bufs[i], flats[i], lists[i], accs[i], sources[i]

    def meet(ai, bi, forward=True, backward=True):
        abuf, _, alist, aacc, adev = data(ai)
        bbuf, brows, blist, bacc, bdev = data(bi)
        col = 0 if ai is None else ai + 1

        if forward:
            tile(abuf, col, aacc, alist[0, bdev], bbuf, brows, bacc, blist[1, adev])
        if backward:
            tile(abuf, col, aacc, alist[1, bdev], bbuf, brows, bacc, blist[0, adev])

    def local(lo, hi):
        def some(i, carry):
            for n in range(5):
                v = i * 5 + n
                k = jnp.where(v >= 4, 1, 0) + jnp.where(v >= 7, 1, 0) + jnp.where(v >= 9, 1, 0)
                l = v - 3 * jnp.where(v >= 4, 1, 0) - 2 * jnp.where(v >= 7, 1, 0) - jnp.where(v >= 9, 1, 0)
                tile(own, 0, accs[9], k, own, flats[9], accs[9], l, same=True)
            return carry

        lax.fori_loop(lo, hi, some, 0)

    def have_meta(i):
        landed(metas[i], meta_recv.at[i])

    def list_copy(i):
        return pltpu.make_async_copy(metas[i].at[pl.ds(8, 8)], lists[i], list_sem.at[i])

    def use_meta(i):
        list_copy(i).start()
        make_rows(metas[i], i)
        if i < 3:
            make_cols(metas[i], i + 1)

    def set_source(points, extra):
        for b in range(4):
            rhs[b * BLOCK:(b + 1) * BLOCK, :LANES] = points[b]
            keep = (lane_ids < 64) if b < 2 else (lane_ids >= 64)
            rhs[b * BLOCK:(b + 1) * BLOCK, LANES:] = jnp.where(keep, extra[b % 2].astype(jnp.float32), 0.0).astype(jnp.bfloat16)

    def add_source(label_ref, lo, hi, mode):
        labels = label_ref[...]
        ys, zs, es = (labels // 256) % 4, (labels // 64) % 4, (labels // 32) % 2
        order = (es * 2048 + jnp.where(es == 0, zs, ys) * 512 + jnp.where(es == 0, ys, zs) * 128 + (labels // 1024) * 32
                 + labels % 32)

        def chunk(i, carry):
            m = lax.rem(i + 2 * other, 4)
            ids = lax.broadcasted_iota(jnp.int32, (ROWS, LANES), 0) + m * ROWS
            hot = jnp.concatenate(
                [jnp.where(order[r:r + 1, :] == ids, 1.0, 0.0).astype(jnp.bfloat16) for r in range(8)], axis=1)
            total = jnp.dot(hot, rhs[...], preferred_element_type=jnp.float32)
            if mode != "first":
                total = total + sums[m]
            if mode != "last":
                sums[m] = total
            else:
                extra = total[:, LANES:]
                extra = extra + pltpu.roll(extra, 64, 1)
                for b in range(32):
                    place_ = (m // 2, 2 * lax.rem(m, 2) + b // 16, (b // 4) % 4, b % 4)
                    cores[(*place_, slice(0, 32))] = total[b * 32:b * 32 + 32, :LANES]
                    cores[(*place_, slice(32, 48))] = jnp.where(
                        lane_ids[:16] < 64, extra[b * 32:b * 32 + 16], extra[b * 32 + 16:b * 32 + 32])
            return carry

        lax.fori_loop(lo, hi, chunk, 0)

    def ring(i):
        return lax.rem(main + i, 4)

    def centroid_send(src, dst, i, device):
        go(remote(src, dst, c_send.at[i], c_recv.at[i], device))

    owners = sorted([(i, k) for k in range(4) for i in range(4) if i or k], key=lambda o: -(min(o[0], 4 - o[0]) + min(o[1], 4 - o[1])))

    def finish_centroids():
        quarters = []
        for q in range(4):
            step = lax.rem(group - q + 4, 4)
            quarters.append(in_last[step, 0] + in_last[step, 1] + in_last[step, 2] + in_last[step, 3])
        tiles = [quarters[q][0:32] for q in range(4)]
        low = lane_ids[:16] < 64
        for t in range(2):
            even, odd = quarters[2 * t][32:48], quarters[2 * t + 1][32:48]
            tiles.append(jnp.concatenate([jnp.where(low, even, pltpu.roll(odd, 64, 1)),
                                          jnp.where(low, pltpu.roll(even, 64, 1), odd)], axis=0))
        squares = tiles[0] * tiles[0]
        for tile_values in tiles[1:]:
            squares = squares + tile_values * tile_values
        scale = lax.rsqrt(jnp.sum(squares, axis=-1, keepdims=True) / 768.0 + 1e-06)
        for c in range(SLICES):
            centroids_out[:, c * LANES:(c + 1) * LANES] = tiles[c] * scale

    def give_back(i):
        go(remote(accs[i], result_in.at[i], res_send.at[i], res_recv.at[i], at(sources[i])))

    def source(i):
        landed(xmeta.at[i], x_recv.at[i, 0])
        landed(xa.at[i], x_recv.at[i, 1])
        landed(xp.at[i], x_recv.at[i, 2])
        set_source(xa.at[i], xp.at[i])

    own_list.wait()
    have_meta(M3)
    meta_go(5)
    have_meta(10)
    meta_go(6)
    have_meta(M1)
    meta_go(7)
    meta_go(8)
    set_source(own.at[group], halves.at[group])
    add_source(lab_in, 0, 4, "first")
    have_meta(M2)
    meta_go(9)
    for i in (X1, X2, P0, P1, P3):
        have_meta(i)
    for i in (M1, M2, M3, X1, X2, P0, P1, P3):
        use_meta(i)
    arrive("o", 0)
    send("f", 0)
    arrive("x", 0)
    send("y", 0)
    mate_copies(1)
    send("h", 2)
    have_meta(P2)
    use_meta(P2)
    local(0, 2)
    source(0)
    add_source(xmeta.at[0], 0, 4, "add")
    arrive("o", 1)
    send("f", 1)
    arrive("x", 1)
    send("y", 1)
    source(2)
    add_source(xmeta.at[2], 0, 4, "add")
    arrive("o", 2)
    send("f", 2)
    share(M1, 0, 6, 1)
    source(1)
    add_source(xmeta.at[1], 0, 2, "last")
    centroid_send(cores.at[other], from_core, 0, partner)
    add_source(xmeta.at[1], 2, 4, "last")
    landed(from_core, c_recv.at[0])
    for i in range(4):
        cores[core, i] = cores[core, i] + from_core[i]
    centroid_send(cores.at[core, ring(2), pl.ds(0, 2)], in_f, 1, forth)
    centroid_send(cores.at[core, ring(2), pl.ds(2, 2)], in_b, 2, back)
    for i in range(9):
        list_copy(i).wait()
    shared_arrival(0)
    meet(None, P0, backward=False)
    meet(M1, P0, backward=False)
    meet(None, M1)
    arrive("x", 2)
    send("y", 2)
    arrive("f", 0)
    send("g", 0)
    meet(None, X1)
    meet(M1, X1)
    arrive("f", 1)
    send("g", 1)
    landed(in_b, c_recv.at[2])
    cores[core, ring(3), 2:4] = cores[core, ring(3), 2:4] + in_b[...]
    centroid_send(cores.at[core, ring(3)], in2_b, 4, back)
    arrive("y", 0)
    landed(in_f, c_recv.at[1])
    cores[core, ring(1), 0:2] = cores[core, ring(1), 0:2] + in_f[...]
    centroid_send(cores.at[core, ring(1)], in2_f, 3, forth)
    shared_arrival(1)
    meet(None, P1, backward=False)
    meet(M1, P1, backward=False)
    early = len(started) - 8
    arrive("f", 2)
    share(M2, 0, 6, 2)
    meet(None, M2, forward=False)
    meet(M2, X1)
    meet(M2, P0, backward=False)
    meet(M2, P1, backward=False)
    arrive("g", 0)
    share(M3, 0, 1, 4)
    arrive("y", 1)
    arrive("h", 2)
    share(M3, 3, 3, 3)
    shared_arrival(2)
    meet(None, P2, backward=False)
    meet(M1, P2, backward=False)
    meet(M2, P2, backward=False)
    drain(early)
    arrive("g", 1)
    share(M3, 1, 2, 5)
    landed(in2_f, c_recv.at[3])
    landed(in2_b, c_recv.at[4])
    cores[core, main] = cores[core, main] + in2_f[...] + in2_b[...]
    in_last[0, 0] = cores[core, main, side, group]
    for i, k in owners:
        target = lax.rem(group + i, 4), lax.rem(side + k, 4)
        centroid_send(cores.at[core, main, target[1], target[0]], in_last.at[i, k], 4 * i + k + 4,
                      (target[0], place(main, side + k, core)))
    arrive("y", 2)
    for i in (None, M1, M2, M3):
        meet(i, X2, forward=False)
    meet(M3, X1)
    for i in (P0, P1, P2):
        meet(M3, i, backward=False)
    for i in (X2, P2, P1, X1, P0):
        give_back(i)
    shared_arrival(3)
    for i in (M3, M2, M1, None):
        meet(i, P3, backward=False)
    for i in (M2, P3, M1, M3):
        give_back(i)
    for i, k in owners:
        landed(in_last.at[i, k], c_recv.at[4 * i + k + 4])
    finish_centroids()
    best = jnp.maximum(accs[9][...], 0.0)
    for i in range(9):
        remote(result_in.at[i], result_in.at[i], res_send.at[i], res_recv.at[i], partner).wait_recv()
        best = jnp.maximum(best, result_in[i])
    scores_out[...] = best
    drain(len(started))


def exchange(embeddings, labels, ranking, send_list, pair_list):
    dataset = pltpu.VMEM((SLICES, 4, BLOCK, LANES), jnp.bfloat16)
    dma = pltpu.SemaphoreType.DMA
    f32, bf16, i32 = jnp.float32, jnp.bfloat16, jnp.int32
    return pl.pallas_call(
        kernel,
        out_shape=(jax.ShapeDtypeStruct((8, LANES), f32), jax.ShapeDtypeStruct((32, SLICES * LANES), f32)),
        in_specs=[pl.BlockSpec(memory_space=pl.ANY)] * 5,
        out_specs=(pl.BlockSpec(memory_space=pltpu.VMEM), pl.BlockSpec(memory_space=pltpu.VMEM)),
        scratch_shapes=[dataset] * 10
        + [pltpu.VMEM((16, LANES), i32)] * 11
        + [pltpu.SMEM((8, LANES), i32)] * 10
        + [pltpu.VMEM((4, BLOCK, LANES), i32)] * 4
        + [pltpu.VMEM((8, LANES), f32)] * 10
        + [pltpu.VMEM((4, 8, BLOCK), i32)] * 10
        + [pltpu.VMEM((9, 8, LANES), f32),
           pltpu.VMEM((4, 2, BLOCK, LANES), bf16),
           pltpu.VMEM((3, 4, BLOCK, LANES), bf16),
           pltpu.VMEM((3, 2, BLOCK, LANES), bf16),
           pltpu.VMEM((3, 8, LANES), i32),
           pltpu.VMEM((ROWS, 2 * LANES), bf16),
           pltpu.VMEM((4, ROWS, 2 * LANES), f32),
           pltpu.VMEM((2, 4, 4, 4, 48, LANES), f32),
           pltpu.VMEM((4, 4, 4, 48, LANES), f32),
           pltpu.VMEM((2, 4, 48, LANES), f32),
           pltpu.VMEM((2, 4, 48, LANES), f32),
           pltpu.VMEM((4, 4, 48, LANES), f32),
           pltpu.VMEM((4, 4, 48, LANES), f32),
           pltpu.VMEM((4, 4, 48, LANES), f32),
           dma((18,)), dma((18,)), dma((6,)), dma((4,)),
           dma((10,)), dma((11,)), dma((10,)), dma((9,)), dma((9,)), dma((3, 3)), dma((3, 3)), dma((20,)), dma((20,)),
           pltpu.VMEM((ROWS, SLICES * LANES), bf16), pltpu.VMEM((8, LANES), i32), pltpu.VMEM((8, LANES), i32),
           pltpu.VMEM((1, 32), i32), pltpu.VMEM((1, 32), i32), dma((5,))],
        compiler_params=pltpu.CompilerParams(collective_id=0, has_side_effects=True, vmem_limit_bytes=60 * 1024 * 1024),
    )(embeddings, labels.reshape(8, LANES), ranking.reshape(8, LANES), send_list, pair_list)


def store_kernel(scores_in, centroids_in, scores_out, centroids_out):
    scores_out[...] = jnp.maximum(scores_in[...], 0.0)
    centroids_out[...] = centroids_in[...]


def store(scores, centroids):
    return pl.pallas_call(
        store_kernel,
        out_shape=(jax.ShapeDtypeStruct(scores.shape, scores.dtype), jax.ShapeDtypeStruct(centroids.shape, centroids.dtype)),
        in_specs=[pl.BlockSpec(memory_space=pltpu.VMEM)] * 2,
        out_specs=(pl.BlockSpec(memory_space=pltpu.VMEM), pl.BlockSpec(memory_space=pltpu.VMEM)),
    )(scores, centroids)


def body(embeddings, labels, ranking, send_list, pair_list):
    scores, centroids = exchange(embeddings, labels, ranking, send_list, pair_list)
    scores, centroids = store(scores, centroids)
    return (scores.reshape(ROWS), centroids)


def solution(mesh):
    return jax.shard_map(
        body,
        mesh=mesh,
        in_specs=(
            P(("group", "dev"), None),
            P(("group", "dev")),
            P(("group", "dev")),
            P(("group", "dev"), None),
            P(("group", "dev"), None),
        ),
        out_specs=(P(("group", "dev")), P(("group", "dev"), None)),
        check_vma=False,
    )
```

```python
import jax
import jax.numpy as jnp
from jax import lax
from jax.experimental import pallas as pl
from jax.experimental.pallas import tpu as pltpu
from jax.sharding import PartitionSpec as P

K = 4096
BLOCK = 256
ROWS = 1024
SLICES = 6
LANES = 128
LOW = -2.0
RANKS = 131072
MESH = pl.DeviceIdType.MESH
M1, M2, M3, X1, X2, P0, P1, P2, P3 = range(9)
PARTS = ((0, 1), (1, 2), (3, 3))
SIDE_ORDER = (2, 1, 3, 0)


def kernel(emb_hbm, lab_hbm, rank_hbm, send_hbm, pair_hbm, scores_hbm, centroids_hbm,
           own, m1, m2, m3, x1, x2, p0, p1, p2, p3, *rest):
    metas = rest[0:11]
    lists = rest[11:21]
    cols = rest[21:25]
    accs = rest[25:35]
    flats = rest[35:45]
    own_meta = metas[9]
    (result_in, halves, xa, xp, xmeta, rhs, sums, cores, from_core, in_f, in_b, in2_f, in2_b, in_last,
     q_send, q_recv, d_send, d_recv, meta_send, meta_recv, list_sem, res_send, res_recv,
     x_send, x_recv, c_send, c_recv, emb, lab_in, rank_in, send_in, pair_in, in_sem,
     scores_out, centroids_out, out_sem) = rest[45:]
    bufs = (m1, m2, m3, x1, x2, p0, p1, p2, p3)
    loads = [pltpu.make_async_copy(src, dst, in_sem.at[i]) for i, (src, dst) in enumerate(
        ((emb_hbm, emb), (lab_hbm, lab_in), (rank_hbm, rank_in), (send_hbm, send_in), (pair_hbm, pair_in)))]
    for copy in loads:
        copy.start()
    group = lax.axis_index("group")
    me = lax.axis_index("dev")
    core = lax.rem(me, 2)
    y, z = me // 8, lax.rem(me // 2, 4)
    main = jnp.where(core == 0, z, y)
    side = jnp.where(core == 0, y, z)
    def place(u, w, e):
        return lax.rem(u, 4) * (2 + 6 * e) + lax.rem(w, 4) * (8 - 6 * e) + e

    def at(index):
        return (group, index)

    other = 1 - core
    sources = [place(main + 1, side, core), place(main + 2, side, core), place(main + 3, side, core),
               place(main, side + 3, core), place(main, side + 2, core),
               place(side, main, other), place(side + 1, main, other), place(side + 2, main, other), place(side + 3, main, other)]
    back = at(place(main + 3, side, core))
    forth = at(place(main + 1, side, core))
    along = at(place(main, side + 1, core))
    partner = at(place(side, main, other))

    behind = at(place(main, side + 3, core))
    mates = [(lax.rem(group + i, 4), me) for i in (1, 2, 3)]

    barrier = pltpu.get_barrier_semaphore()
    for device in [forth, back, along, behind, partner] + mates:
        pl.semaphore_signal(barrier, inc=1, device_id=device, device_id_type=MESH)

    for copy in loads[1:]:
        copy.wait()
    own_meta[0:8, :] = lab_in[...] * RANKS + rank_in[...]
    own_meta[8:9, 0:32] = send_in[...]
    own_meta[9:10, 0:32] = pair_in[...]

    def normalize(i, carry):
        rows = pl.ds(pl.multiple_of(i * 128, 128), 128)
        values = emb[rows, :].astype(jnp.float32)
        scaled = values * lax.rsqrt(jnp.sum(values * values, axis=-1, keepdims=True) + 1e-06)
        unit = scaled.astype(jnp.bfloat16)
        for c in range(SLICES):
            own[c, i // 2, pl.ds(pl.multiple_of(lax.rem(i, 2) * 128, 128), 128), :] = unit[:, c * LANES:(c + 1) * LANES]
        return carry

    loads[0].wait()
    lax.fori_loop(0, 8, normalize, 0)
    lane_ids = lax.broadcasted_iota(jnp.int32, (BLOCK, LANES), 1)

    for t in range(2):
        for b in range(2):
            low = own[4 + t, b].astype(jnp.float32)
            high = own[4 + t, b + 2].astype(jnp.float32)
            halves[2 * t, b] = jnp.where(lane_ids < 64, low, pltpu.roll(high, 64, 1)).astype(jnp.bfloat16)
            halves[2 * t + 1, b] = jnp.where(lane_ids < 64, pltpu.roll(low, 64, 1), high).astype(jnp.bfloat16)
    pl.semaphore_wait(barrier, 8)

    started = []

    def remote(src, dst, send, recv, device):
        return pltpu.make_async_remote_copy(src_ref=src, dst_ref=dst, send_sem=send, recv_sem=recv, device_id=device,
                                            device_id_type=MESH)

    def go(copy):
        copy.start()
        started.append(copy)

    def drain(count):
        for copy in started[:count]:
            copy.wait_send()
        del started[:count]

    legs = {"o": (own, m1, back, 0), "f": (m1, m2, back, 3), "g": (m2, m3, back, 6), "h": (own, m3, forth, 9),
            "x": (own, x1, along, 12), "y": (x1, x2, along, 15)}

    def send(leg, part):
        src, dst, device, sem = legs[leg]
        piece = pl.ds(*PARTS[part])
        go(remote(src.at[piece], dst.at[piece], q_send.at[sem + part], q_recv.at[sem + part], device))

    def arrive(leg, part):
        _, dst, _, sem = legs[leg]
        landed(dst.at[pl.ds(*PARTS[part])], q_recv.at[sem + part])

    def landed(dst, recv):
        remote(dst, dst, res_send.at[0], recv, partner).wait_recv()

    meta_routes = [(9, M1, back), (9, M3, forth), (9, X1, along), (9, 10, behind), (9, P0, partner),
                   (M3, M2, forth), (10, X2, behind), (M1, P1, partner), (M3, P3, partner), (M2, P2, partner)]

    def meta_go(i):
        src, dst, device = meta_routes[i]
        go(remote(metas[src], metas[dst], meta_send.at[i], meta_recv.at[dst], device))

    def mate_copies(i):
        quarter = lax.rem(group + 1 + i, 4)
        go(remote(lab_in, xmeta.at[i], x_send.at[i, 0], x_recv.at[i, 0], mates[i]))
        go(remote(own.at[quarter], xa.at[i], x_send.at[i, 1], x_recv.at[i, 1], mates[i]))
        go(remote(halves.at[quarter], xp.at[i], x_send.at[i, 2], x_recv.at[i, 2], mates[i]))

    for i in range(5):
        meta_go(i)
    send("o", 0)
    send("x", 0)
    mate_copies(0)
    mate_copies(2)
    send("o", 1)
    send("x", 1)
    send("o", 2)
    send("x", 2)
    go(remote(own, p0, d_send.at[0], d_recv.at[0], partner))

    def share(which, first, count, slot):
        src, dst = bufs[which], bufs[which + P1]
        go(remote(src.at[pl.ds(first, count)], dst.at[pl.ds(first, count)], d_send.at[slot], d_recv.at[which + 1], partner))

    def shared_arrival(i):
        dst = (p0, p1, p2, p3)[i]
        remote(dst, dst, d_send.at[0], d_recv.at[i], partner).wait_recv()

    def make_cols(meta, i):
        for r in range(8):
            row = jnp.broadcast_to(meta[r:r + 1, :], (LANES, LANES))
            cols[i][r // 2, (r % 2) * LANES:(r % 2 + 1) * LANES, :] = row.T

    def make_rows(meta, i):
        keys = meta[0:8, :]
        floors = keys & (-RANKS)
        for r in range(8):
            lanes = slice((r % 2) * LANES, (r % 2 + 1) * LANES)
            flats[i][r // 2, 0:1, lanes] = keys[r:r + 1, :]
            flats[i][r // 2, 1:2, lanes] = floors[r:r + 1, :]

    make_cols(own_meta, 0)
    make_rows(own_meta, 9)
    own_list = pltpu.make_async_copy(own_meta.at[pl.ds(8, 8)], lists[9], list_sem.at[9])
    own_list.start()
    for acc in accs:
        acc[...] = jnp.full((8, LANES), LOW, jnp.float32)
    row_ids = lax.broadcasted_iota(jnp.int32, (8, LANES), 0)

    def update(acc, block, row):
        spread = jnp.where(lax.rem(row_ids, 2) == 0, row[:, :LANES], row[:, LANES:])
        acc[...] = jnp.where(row_ids // 2 == block, jnp.maximum(acc[...], spread), acc[...])

    def tile(abuf, acol, aacc, a, bbuf, brows, bacc, b, same=False):
        left = jnp.concatenate([abuf[c, a] for c in range(SLICES)], axis=1)
        right = jnp.concatenate([bbuf[c, b] for c in range(SLICES)], axis=1)
        similar = lax.dot_general(left, right, (((1,), (1,)), ((), ())), preferred_element_type=jnp.float32)
        akey = cols[acol][a]
        afloor = akey & (-RANKS)
        brow = brows[b]
        for_a, for_b = None, []
        for h in range(2):
            lanes = slice(h * LANES, (h + 1) * LANES)
            bkey, bfloor = brow[0:1, lanes], brow[1:2, lanes]
            value = jnp.where(afloor == bfloor, similar[:, lanes], LOW)
            later = bkey < akey
            va = jnp.where(later, value, LOW)
            vb = jnp.where(akey < bkey, value, LOW) if same else jnp.where(later, LOW, value)
            for_a = va if for_a is None else jnp.maximum(for_a, va)
            for_b.append(jnp.max(vb, axis=0, keepdims=True))
        update(aacc, a, jnp.max(for_a.T, axis=0, keepdims=True))
        update(bacc, b, jnp.concatenate(for_b, axis=1))

    def data(i):
        if i is None:
            return own, flats[9], lists[9], accs[9], me
        return bufs[i], flats[i], lists[i], accs[i], sources[i]

    def meet(ai, bi, forward=True, backward=True):
        abuf, _, alist, aacc, adev = data(ai)
        bbuf, brows, blist, bacc, bdev = data(bi)
        col = 0 if ai is None else ai + 1

        if forward:
            tile(abuf, col, aacc, alist[0, bdev], bbuf, brows, bacc, blist[1, adev])
        if backward:
            tile(abuf, col, aacc, alist[1, bdev], bbuf, brows, bacc, blist[0, adev])

    def local(lo, hi):
        def some(i, carry):
            for n in range(5):
                v = i * 5 + n
                k = jnp.where(v >= 4, 1, 0) + jnp.where(v >= 7, 1, 0) + jnp.where(v >= 9, 1, 0)
                l = v - 3 * jnp.where(v >= 4, 1, 0) - 2 * jnp.where(v >= 7, 1, 0) - jnp.where(v >= 9, 1, 0)
                tile(own, 0, accs[9], k, own, flats[9], accs[9], l, same=True)
            return carry

        lax.fori_loop(lo, hi, some, 0)

    def have_meta(i):
        landed(metas[i], meta_recv.at[i])

    def list_copy(i):
        return pltpu.make_async_copy(metas[i].at[pl.ds(8, 8)], lists[i], list_sem.at[i])

    def use_meta(i):
        list_copy(i).start()
        make_rows(metas[i], i)
        if i < 3:
            make_cols(metas[i], i + 1)

    def set_source(points, extra):
        for b in range(4):
            rhs[b * BLOCK:(b + 1) * BLOCK, :LANES] = points[b]
            keep = (lane_ids < 64) if b < 2 else (lane_ids >= 64)
            rhs[b * BLOCK:(b + 1) * BLOCK, LANES:] = jnp.where(keep, extra[b % 2].astype(jnp.float32), 0.0).astype(jnp.bfloat16)

    def add_source(label_ref, lo, hi, mode):
        labels = label_ref[...]
        ys, zs, es = (labels // 256) % 4, (labels // 64) % 4, (labels // 32) % 2
        order = (es * 2048 + jnp.where(es == 0, zs, ys) * 512 + jnp.where(es == 0, ys, zs) * 128 + (labels // 1024) * 32
                 + labels % 32)

        def chunk(i, carry):
            m = lax.rem(i + 2 * other, 4)
            ids = lax.broadcasted_iota(jnp.int32, (ROWS, LANES), 0) + m * ROWS
            hot = jnp.concatenate(
                [jnp.where(order[r:r + 1, :] == ids, 1.0, 0.0).astype(jnp.bfloat16) for r in range(8)], axis=1)
            total = jnp.dot(hot, rhs[...], preferred_element_type=jnp.float32)
            if mode != "first":
                total = total + sums[m]
            if mode != "last":
                sums[m] = total
            else:
                extra = total[:, LANES:]
                extra = extra + pltpu.roll(extra, 64, 1)
                for b in range(32):
                    place_ = (m // 2, 2 * lax.rem(m, 2) + b // 16, (b // 4) % 4, b % 4)
                    cores[(*place_, slice(0, 32))] = total[b * 32:b * 32 + 32, :LANES]
                    cores[(*place_, slice(32, 48))] = jnp.where(
                        lane_ids[:16] < 64, extra[b * 32:b * 32 + 16], extra[b * 32 + 16:b * 32 + 32])
            return carry

        lax.fori_loop(lo, hi, chunk, 0)

    def ring(i):
        return lax.rem(main + i, 4)

    def centroid_send(src, dst, i, device):
        go(remote(src, dst, c_send.at[i], c_recv.at[i], device))

    owners = sorted([(i, k) for k in range(4) for i in range(4) if i or k], key=lambda o: -(min(o[0], 4 - o[0]) + min(o[1], 4 - o[1])))

    def across(k):
        return lax.rem(side + k, 4)

    def to_owners(k):
        landed(in2_f.at[across(k)], c_recv.at[20 + k])
        landed(in2_b.at[across(k)], c_recv.at[24 + k])
        mine = cores.at[core, main, across(k)]
        mine[...] = mine[...] + in2_f[across(k)] + in2_b[across(k)]
        if k == 0:
            in_last[0, 0] = mine[group]
        for i in (2, 1, 3, 0):
            if i or k:
                target = lax.rem(group + i, 4)
                centroid_send(mine.at[target], in_last.at[i, k], 4 * i + k + 4, (target, place(main, side + k, core)))

    def finish_centroids():
        quarters = []
        for q in range(4):
            step = lax.rem(group - q + 4, 4)
            quarters.append(in_last[step, 0] + in_last[step, 1] + in_last[step, 2] + in_last[step, 3])
        tiles = [quarters[q][0:32] for q in range(4)]
        low = lane_ids[:16] < 64
        for t in range(2):
            even, odd = quarters[2 * t][32:48], quarters[2 * t + 1][32:48]
            tiles.append(jnp.concatenate([jnp.where(low, even, pltpu.roll(odd, 64, 1)),
                                          jnp.where(low, pltpu.roll(even, 64, 1), odd)], axis=0))
        squares = tiles[0] * tiles[0]
        for tile_values in tiles[1:]:
            squares = squares + tile_values * tile_values
        scale = lax.rsqrt(jnp.sum(squares, axis=-1, keepdims=True) / 768.0 + 1e-06)
        for c in range(SLICES):
            centroids_out[:, c * LANES:(c + 1) * LANES] = tiles[c] * scale

    def give_back(i):
        go(remote(accs[i], result_in.at[i], res_send.at[i], res_recv.at[i], at(sources[i])))

    def source(i):
        landed(xmeta.at[i], x_recv.at[i, 0])
        landed(xa.at[i], x_recv.at[i, 1])
        landed(xp.at[i], x_recv.at[i, 2])
        set_source(xa.at[i], xp.at[i])

    own_list.wait()
    have_meta(M3)
    meta_go(5)
    have_meta(10)
    meta_go(6)
    have_meta(M1)
    meta_go(7)
    meta_go(8)
    set_source(own.at[group], halves.at[group])
    add_source(lab_in, 0, 4, "first")
    have_meta(M2)
    meta_go(9)
    for i in (X1, X2, P0, P1, P3):
        have_meta(i)
    for i in (M1, M2, M3, X1, X2, P0, P1, P3):
        use_meta(i)
    arrive("o", 0)
    send("f", 0)
    arrive("x", 0)
    send("y", 0)
    mate_copies(1)
    send("h", 2)
    have_meta(P2)
    use_meta(P2)
    local(0, 2)
    source(0)
    add_source(xmeta.at[0], 0, 4, "add")
    arrive("o", 1)
    send("f", 1)
    arrive("x", 1)
    send("y", 1)
    source(2)
    add_source(xmeta.at[2], 0, 4, "add")
    arrive("o", 2)
    send("f", 2)
    share(M1, 0, 6, 1)
    source(1)
    add_source(xmeta.at[1], 0, 2, "last")
    centroid_send(cores.at[other], from_core, 0, partner)
    add_source(xmeta.at[1], 2, 4, "last")
    landed(from_core, c_recv.at[0])
    for i in range(4):
        cores[core, i] = cores[core, i] + from_core[i]
    centroid_send(cores.at[core, ring(2), pl.ds(0, 2)], in_f, 1, forth)
    centroid_send(cores.at[core, ring(2), pl.ds(2, 2)], in_b, 2, back)
    for i in range(9):
        list_copy(i).wait()
    shared_arrival(0)
    meet(None, P0, backward=False)
    meet(M1, P0, backward=False)
    meet(None, M1)
    arrive("x", 2)
    send("y", 2)
    arrive("f", 0)
    send("g", 0)
    meet(None, X1)
    meet(M1, X1)
    arrive("f", 1)
    send("g", 1)
    landed(in_b, c_recv.at[2])
    cores[core, ring(3), 2:4] = cores[core, ring(3), 2:4] + in_b[...]
    for k in SIDE_ORDER:
        centroid_send(cores.at[core, ring(3), across(k)], in2_b.at[across(k)], 24 + k, back)
    arrive("y", 0)
    landed(in_f, c_recv.at[1])
    cores[core, ring(1), 0:2] = cores[core, ring(1), 0:2] + in_f[...]
    for k in SIDE_ORDER:
        centroid_send(cores.at[core, ring(1), across(k)], in2_f.at[across(k)], 20 + k, forth)
    shared_arrival(1)
    meet(None, P1, backward=False)
    meet(M1, P1, backward=False)
    early = len(started) - 8
    arrive("f", 2)
    share(M2, 0, 6, 2)
    meet(None, M2, forward=False)
    meet(M2, X1)
    meet(M2, P0, backward=False)
    meet(M2, P1, backward=False)
    arrive("g", 0)
    share(M3, 0, 1, 4)
    arrive("y", 1)
    arrive("h", 2)
    share(M3, 3, 3, 3)
    shared_arrival(2)
    meet(None, P2, backward=False)
    meet(M1, P2, backward=False)
    meet(M2, P2, backward=False)
    drain(early)
    arrive("g", 1)
    share(M3, 1, 2, 5)
    meet(M3, X1)
    for i in (P0, P1, P2):
        meet(M3, i, backward=False)
    to_owners(2)
    to_owners(1)
    shared_arrival(3)
    for i in (M3, M2, M1, None):
        meet(i, P3, backward=False)
    for i in (P2, P1, P3, X1, P0):
        give_back(i)
    to_owners(3)
    arrive("y", 2)
    for i in (None, M1, M2, M3):
        meet(i, X2, forward=False)
    for i in (X2, M2, M1, M3):
        give_back(i)
    to_owners(0)
    drain(len(started) - 20)
    for i, k in owners:
        landed(in_last.at[i, k], c_recv.at[4 * i + k + 4])
    finish_centroids()
    stores = [pltpu.make_async_copy(src, dst, out_sem.at[i]) for i, (src, dst) in enumerate(
        ((centroids_out, centroids_hbm), (scores_out, scores_hbm)))]
    stores[0].start()
    drain(len(started))
    best = jnp.maximum(accs[9][...], 0.0)
    for i in range(9):
        landed(result_in.at[i], res_recv.at[i])
        best = jnp.maximum(best, result_in[i])
    scores_out[...] = best
    stores[1].start()
    for copy in stores:
        copy.wait()


def exchange(embeddings, labels, ranking, send_list, pair_list):
    dataset = pltpu.VMEM((SLICES, 4, BLOCK, LANES), jnp.bfloat16)
    dma = pltpu.SemaphoreType.DMA
    f32, bf16, i32 = jnp.float32, jnp.bfloat16, jnp.int32
    return pl.pallas_call(
        kernel,
        out_shape=(jax.ShapeDtypeStruct((8, LANES), f32), jax.ShapeDtypeStruct((32, SLICES * LANES), f32)),
        in_specs=[pl.BlockSpec(memory_space=pl.ANY)] * 5,
        out_specs=(pl.BlockSpec(memory_space=pl.ANY), pl.BlockSpec(memory_space=pl.ANY)),
        scratch_shapes=[dataset] * 10
        + [pltpu.VMEM((16, LANES), i32)] * 11
        + [pltpu.SMEM((8, LANES), i32)] * 10
        + [pltpu.VMEM((4, BLOCK, LANES), i32)] * 4
        + [pltpu.VMEM((8, LANES), f32)] * 10
        + [pltpu.VMEM((4, 8, BLOCK), i32)] * 10
        + [pltpu.VMEM((9, 8, LANES), f32),
           pltpu.VMEM((4, 2, BLOCK, LANES), bf16),
           pltpu.VMEM((3, 4, BLOCK, LANES), bf16),
           pltpu.VMEM((3, 2, BLOCK, LANES), bf16),
           pltpu.VMEM((3, 8, LANES), i32),
           pltpu.VMEM((ROWS, 2 * LANES), bf16),
           pltpu.VMEM((4, ROWS, 2 * LANES), f32),
           pltpu.VMEM((2, 4, 4, 4, 48, LANES), f32),
           pltpu.VMEM((4, 4, 4, 48, LANES), f32),
           pltpu.VMEM((2, 4, 48, LANES), f32),
           pltpu.VMEM((2, 4, 48, LANES), f32),
           pltpu.VMEM((4, 4, 48, LANES), f32),
           pltpu.VMEM((4, 4, 48, LANES), f32),
           pltpu.VMEM((4, 4, 48, LANES), f32),
           dma((18,)), dma((18,)), dma((6,)), dma((4,)),
           dma((10,)), dma((11,)), dma((10,)), dma((9,)), dma((9,)), dma((3, 3)), dma((3, 3)), dma((28,)), dma((28,)),
           pltpu.VMEM((ROWS, SLICES * LANES), bf16), pltpu.VMEM((8, LANES), i32), pltpu.VMEM((8, LANES), i32),
           pltpu.VMEM((1, 32), i32), pltpu.VMEM((1, 32), i32), dma((5,)),
           pltpu.VMEM((8, LANES), f32), pltpu.VMEM((32, SLICES * LANES), f32), dma((2,))],
        compiler_params=pltpu.CompilerParams(collective_id=0, has_side_effects=True, vmem_limit_bytes=60 * 1024 * 1024),
    )(embeddings, labels.reshape(8, LANES), ranking.reshape(8, LANES), send_list, pair_list)


def store_kernel(scores_in, centroids_in, scores_out, centroids_out):
    scores_out[...] = jnp.maximum(scores_in[...], 0.0)
    centroids_out[...] = centroids_in[...]


def store(scores, centroids):
    return pl.pallas_call(
        store_kernel,
        out_shape=(jax.ShapeDtypeStruct(scores.shape, scores.dtype), jax.ShapeDtypeStruct(centroids.shape, centroids.dtype)),
        in_specs=[pl.BlockSpec(memory_space=pltpu.VMEM)] * 2,
        out_specs=(pl.BlockSpec(memory_space=pltpu.VMEM), pl.BlockSpec(memory_space=pltpu.VMEM)),
    )(scores, centroids)


def body(embeddings, labels, ranking, send_list, pair_list):
    scores, centroids = exchange(embeddings, labels, ranking, send_list, pair_list)
    scores, centroids = store(scores, centroids)
    return (scores.reshape(ROWS), centroids)


def solution(mesh):
    return jax.shard_map(
        body,
        mesh=mesh,
        in_specs=(
            P(("group", "dev"), None),
            P(("group", "dev")),
            P(("group", "dev")),
            P(("group", "dev"), None),
            P(("group", "dev"), None),
        ),
        out_specs=(P(("group", "dev")), P(("group", "dev"), None)),
        check_vma=False,
    )
```

```python
import jax
import jax.numpy as jnp
from jax import lax
from jax.experimental import pallas as pl
from jax.experimental.pallas import tpu as pltpu
from jax.sharding import PartitionSpec as P

K = 4096
BLOCK = 256
ROWS = 1024
SLICES = 6
LANES = 128
LOW = -2.0
RANKS = 131072
MESH = pl.DeviceIdType.MESH
M1, M2, M3, X1, X2, P0, P1, P2, P3 = range(9)
PARTS = ((0, 1), (1, 2), (3, 3))
SIDE_ORDER = (1, 2, 3, 0)


def kernel(emb_hbm, lab_hbm, rank_hbm, send_hbm, pair_hbm, scores_hbm, centroids_hbm,
           own, m1, m2, m3, x1, x2, p0, p1, p2, p3, *rest):
    metas = rest[0:11]
    lists = rest[11:21]
    cols = rest[21:25]
    accs = rest[25:35]
    flats = rest[35:45]
    own_meta = metas[9]
    (result_in, halves, xa, xp, xmeta, rhs, sums, cores, from_core, in_f, in_b, in2_f, in2_b, in_last,
     q_send, q_recv, d_send, d_recv, meta_send, meta_recv, list_sem, res_send, res_recv,
     x_send, x_recv, c_send, c_recv, emb, lab_in, rank_in, send_in, pair_in, in_sem,
     scores_out, centroids_out, out_sem) = rest[45:]
    bufs = (m1, m2, m3, x1, x2, p0, p1, p2, p3)
    loads = [pltpu.make_async_copy(src, dst, in_sem.at[i]) for i, (src, dst) in enumerate(
        ((emb_hbm, emb), (lab_hbm, lab_in), (rank_hbm, rank_in), (send_hbm, send_in), (pair_hbm, pair_in)))]
    for copy in loads:
        copy.start()
    group = lax.axis_index("group")
    me = lax.axis_index("dev")
    core = lax.rem(me, 2)
    y, z = me // 8, lax.rem(me // 2, 4)
    main = jnp.where(core == 0, z, y)
    side = jnp.where(core == 0, y, z)
    def place(u, w, e):
        return lax.rem(u, 4) * (2 + 6 * e) + lax.rem(w, 4) * (8 - 6 * e) + e

    def at(index):
        return (group, index)

    other = 1 - core
    sources = [place(main + 1, side, core), place(main + 2, side, core), place(main + 3, side, core),
               place(main, side + 3, core), place(main, side + 2, core),
               place(side, main, other), place(side + 1, main, other), place(side + 2, main, other), place(side + 3, main, other)]
    back = at(place(main + 3, side, core))
    forth = at(place(main + 1, side, core))
    along = at(place(main, side + 1, core))
    partner = at(place(side, main, other))

    behind = at(place(main, side + 3, core))
    mates = [(lax.rem(group + i, 4), me) for i in (1, 2, 3)]

    barrier = pltpu.get_barrier_semaphore()
    for device in [forth, back, along, behind, partner] + mates:
        pl.semaphore_signal(barrier, inc=1, device_id=device, device_id_type=MESH)

    for copy in loads[1:]:
        copy.wait()
    own_meta[0:8, :] = lab_in[...] * RANKS + rank_in[...]
    own_meta[8:9, 0:32] = send_in[...]
    own_meta[9:10, 0:32] = pair_in[...]

    def normalize(i, carry):
        rows = pl.ds(pl.multiple_of(i * 128, 128), 128)
        values = emb[rows, :].astype(jnp.float32)
        scaled = values * lax.rsqrt(jnp.sum(values * values, axis=-1, keepdims=True) + 1e-06)
        unit = scaled.astype(jnp.bfloat16)
        for c in range(SLICES):
            own[c, i // 2, pl.ds(pl.multiple_of(lax.rem(i, 2) * 128, 128), 128), :] = unit[:, c * LANES:(c + 1) * LANES]
        return carry

    loads[0].wait()
    lax.fori_loop(0, 8, normalize, 0)
    lane_ids = lax.broadcasted_iota(jnp.int32, (BLOCK, LANES), 1)

    for t in range(2):
        for b in range(2):
            low = own[4 + t, b].astype(jnp.float32)
            high = own[4 + t, b + 2].astype(jnp.float32)
            halves[2 * t, b] = jnp.where(lane_ids < 64, low, pltpu.roll(high, 64, 1)).astype(jnp.bfloat16)
            halves[2 * t + 1, b] = jnp.where(lane_ids < 64, pltpu.roll(low, 64, 1), high).astype(jnp.bfloat16)
    pl.semaphore_wait(barrier, 8)

    started = []

    def remote(src, dst, send, recv, device):
        return pltpu.make_async_remote_copy(src_ref=src, dst_ref=dst, send_sem=send, recv_sem=recv, device_id=device,
                                            device_id_type=MESH)

    def go(copy):
        copy.start()
        started.append(copy)

    def drain(count):
        for copy in started[:count]:
            copy.wait_send()
        del started[:count]

    legs = {"o": (own, m1, back, 0), "f": (m1, m2, back, 3), "g": (m2, m3, back, 6), "h": (own, m3, forth, 9),
            "x": (own, x1, along, 12), "y": (x1, x2, along, 15)}

    def send(leg, part):
        src, dst, device, sem = legs[leg]
        piece = pl.ds(*PARTS[part])
        go(remote(src.at[piece], dst.at[piece], q_send.at[sem + part], q_recv.at[sem + part], device))

    def arrive(leg, part):
        _, dst, _, sem = legs[leg]
        landed(dst.at[pl.ds(*PARTS[part])], q_recv.at[sem + part])

    def landed(dst, recv):
        remote(dst, dst, res_send.at[0], recv, partner).wait_recv()

    meta_routes = [(9, M1, back), (9, M3, forth), (9, X1, along), (9, 10, behind), (9, P0, partner),
                   (M3, M2, forth), (10, X2, behind), (M1, P1, partner), (M3, P3, partner), (M2, P2, partner)]

    def meta_go(i):
        src, dst, device = meta_routes[i]
        go(remote(metas[src], metas[dst], meta_send.at[i], meta_recv.at[dst], device))

    def mate_copies(i):
        quarter = lax.rem(group + 1 + i, 4)
        go(remote(lab_in, xmeta.at[i], x_send.at[i, 0], x_recv.at[i, 0], mates[i]))
        go(remote(own.at[quarter], xa.at[i], x_send.at[i, 1], x_recv.at[i, 1], mates[i]))
        go(remote(halves.at[quarter], xp.at[i], x_send.at[i, 2], x_recv.at[i, 2], mates[i]))

    for i in range(5):
        meta_go(i)
    send("o", 0)
    send("x", 0)
    mate_copies(0)
    mate_copies(2)
    send("o", 1)
    send("x", 1)
    send("o", 2)
    send("x", 2)
    go(remote(own, p0, d_send.at[0], d_recv.at[0], partner))

    def share(which, first, count, slot):
        src, dst = bufs[which], bufs[which + P1]
        go(remote(src.at[pl.ds(first, count)], dst.at[pl.ds(first, count)], d_send.at[slot], d_recv.at[which + 1], partner))

    def shared_arrival(i):
        dst = (p0, p1, p2, p3)[i]
        remote(dst, dst, d_send.at[0], d_recv.at[i], partner).wait_recv()

    def make_cols(meta, i):
        for r in range(8):
            row = jnp.broadcast_to(meta[r:r + 1, :], (LANES, LANES))
            cols[i][r // 2, (r % 2) * LANES:(r % 2 + 1) * LANES, :] = row.T

    def make_rows(meta, i):
        keys = meta[0:8, :]
        floors = keys & (-RANKS)
        for r in range(8):
            lanes = slice((r % 2) * LANES, (r % 2 + 1) * LANES)
            flats[i][r // 2, 0:1, lanes] = keys[r:r + 1, :]
            flats[i][r // 2, 1:2, lanes] = floors[r:r + 1, :]

    make_cols(own_meta, 0)
    make_rows(own_meta, 9)
    own_list = pltpu.make_async_copy(own_meta.at[pl.ds(8, 8)], lists[9], list_sem.at[9])
    own_list.start()
    for acc in accs:
        acc[...] = jnp.full((8, LANES), LOW, jnp.float32)
    row_ids = lax.broadcasted_iota(jnp.int32, (8, LANES), 0)

    def update(acc, block, row):
        spread = jnp.where(lax.rem(row_ids, 2) == 0, row[:, :LANES], row[:, LANES:])
        acc[...] = jnp.where(row_ids // 2 == block, jnp.maximum(acc[...], spread), acc[...])

    def tile(abuf, acol, aacc, a, bbuf, brows, bacc, b, same=False):
        left = jnp.concatenate([abuf[c, a] for c in range(SLICES)], axis=1)
        right = jnp.concatenate([bbuf[c, b] for c in range(SLICES)], axis=1)
        similar = lax.dot_general(left, right, (((1,), (1,)), ((), ())), preferred_element_type=jnp.float32)
        akey = cols[acol][a]
        afloor = akey & (-RANKS)
        brow = brows[b]
        for_a, for_b = None, []
        for h in range(2):
            lanes = slice(h * LANES, (h + 1) * LANES)
            bkey, bfloor = brow[0:1, lanes], brow[1:2, lanes]
            value = jnp.where(afloor == bfloor, similar[:, lanes], LOW)
            later = bkey < akey
            va = jnp.where(later, value, LOW)
            vb = jnp.where(akey < bkey, value, LOW) if same else jnp.where(later, LOW, value)
            for_a = va if for_a is None else jnp.maximum(for_a, va)
            for_b.append(jnp.max(vb, axis=0, keepdims=True))
        update(aacc, a, jnp.max(for_a.T, axis=0, keepdims=True))
        update(bacc, b, jnp.concatenate(for_b, axis=1))

    def data(i):
        if i is None:
            return own, flats[9], lists[9], accs[9], me
        return bufs[i], flats[i], lists[i], accs[i], sources[i]

    def meet(ai, bi, forward=True, backward=True):
        abuf, _, alist, aacc, adev = data(ai)
        bbuf, brows, blist, bacc, bdev = data(bi)
        col = 0 if ai is None else ai + 1

        if forward:
            tile(abuf, col, aacc, alist[0, bdev], bbuf, brows, bacc, blist[1, adev])
        if backward:
            tile(abuf, col, aacc, alist[1, bdev], bbuf, brows, bacc, blist[0, adev])

    def local(lo, hi):
        def some(i, carry):
            for n in range(5):
                v = i * 5 + n
                k = jnp.where(v >= 4, 1, 0) + jnp.where(v >= 7, 1, 0) + jnp.where(v >= 9, 1, 0)
                l = v - 3 * jnp.where(v >= 4, 1, 0) - 2 * jnp.where(v >= 7, 1, 0) - jnp.where(v >= 9, 1, 0)
                tile(own, 0, accs[9], k, own, flats[9], accs[9], l, same=True)
            return carry

        lax.fori_loop(lo, hi, some, 0)

    def have_meta(i):
        landed(metas[i], meta_recv.at[i])

    def list_copy(i):
        return pltpu.make_async_copy(metas[i].at[pl.ds(8, 8)], lists[i], list_sem.at[i])

    def use_meta(i):
        list_copy(i).start()
        make_rows(metas[i], i)
        if i < 3:
            make_cols(metas[i], i + 1)

    def set_source(points, extra):
        for b in range(4):
            rhs[b * BLOCK:(b + 1) * BLOCK, :LANES] = points[b]
            keep = (lane_ids < 64) if b < 2 else (lane_ids >= 64)
            rhs[b * BLOCK:(b + 1) * BLOCK, LANES:] = jnp.where(keep, extra[b % 2].astype(jnp.float32), 0.0).astype(jnp.bfloat16)

    def add_source(label_ref, lo, hi, mode):
        labels = label_ref[...]
        ys, zs, es = (labels // 256) % 4, (labels // 64) % 4, (labels // 32) % 2
        order = (es * 2048 + jnp.where(es == 0, zs, ys) * 512 + jnp.where(es == 0, ys, zs) * 128 + (labels // 1024) * 32
                 + labels % 32)

        def chunk(i, carry):
            m = lax.rem(i + 2 * other, 4)
            ids = lax.broadcasted_iota(jnp.int32, (ROWS, LANES), 0) + m * ROWS
            hot = jnp.concatenate(
                [jnp.where(order[r:r + 1, :] == ids, 1.0, 0.0).astype(jnp.bfloat16) for r in range(8)], axis=1)
            total = jnp.dot(hot, rhs[...], preferred_element_type=jnp.float32)
            if mode != "first":
                total = total + sums[m]
            if mode != "last":
                sums[m] = total
            else:
                extra = total[:, LANES:]
                extra = extra + pltpu.roll(extra, 64, 1)
                for b in range(32):
                    place_ = (m // 2, 2 * lax.rem(m, 2) + b // 16, (b // 4) % 4, b % 4)
                    cores[(*place_, slice(0, 32))] = total[b * 32:b * 32 + 32, :LANES]
                    cores[(*place_, slice(32, 48))] = jnp.where(
                        lane_ids[:16] < 64, extra[b * 32:b * 32 + 16], extra[b * 32 + 16:b * 32 + 32])
            return carry

        lax.fori_loop(lo, hi, chunk, 0)

    def ring(i):
        return lax.rem(main + i, 4)

    def centroid_send(src, dst, i, device):
        go(remote(src, dst, c_send.at[i], c_recv.at[i], device))

    owners = sorted([(i, k) for k in range(4) for i in range(4) if i or k], key=lambda o: -(min(o[0], 4 - o[0]) + min(o[1], 4 - o[1])))

    def across(k):
        return lax.rem(side + k, 4)

    def to_owners(k):
        landed(in2_f.at[across(k)], c_recv.at[20 + k])
        landed(in2_b.at[across(k)], c_recv.at[24 + k])
        mine = cores.at[core, main, across(k)]
        mine[...] = mine[...] + in2_f[across(k)] + in2_b[across(k)]
        if k == 0:
            in_last[0, 0] = mine[group]
        for i in (2, 1, 3, 0):
            if i or k:
                target = lax.rem(group + i, 4)
                centroid_send(mine.at[target], in_last.at[i, k], 4 * i + k + 4, (target, place(main, side + k, core)))

    def finish_centroids():
        quarters = []
        for q in range(4):
            step = lax.rem(group - q + 4, 4)
            quarters.append(in_last[step, 0] + in_last[step, 1] + in_last[step, 2] + in_last[step, 3])
        tiles = [quarters[q][0:32] for q in range(4)]
        low = lane_ids[:16] < 64
        for t in range(2):
            even, odd = quarters[2 * t][32:48], quarters[2 * t + 1][32:48]
            tiles.append(jnp.concatenate([jnp.where(low, even, pltpu.roll(odd, 64, 1)),
                                          jnp.where(low, pltpu.roll(even, 64, 1), odd)], axis=0))
        squares = tiles[0] * tiles[0]
        for tile_values in tiles[1:]:
            squares = squares + tile_values * tile_values
        scale = lax.rsqrt(jnp.sum(squares, axis=-1, keepdims=True) / 768.0 + 1e-06)
        for c in range(SLICES):
            centroids_out[:, c * LANES:(c + 1) * LANES] = tiles[c] * scale

    def give_back(i):
        go(remote(accs[i], result_in.at[i], res_send.at[i], res_recv.at[i], at(sources[i])))

    def source(i):
        landed(xmeta.at[i], x_recv.at[i, 0])
        landed(xa.at[i], x_recv.at[i, 1])
        landed(xp.at[i], x_recv.at[i, 2])
        set_source(xa.at[i], xp.at[i])

    own_list.wait()
    have_meta(M3)
    meta_go(5)
    have_meta(10)
    meta_go(6)
    have_meta(M1)
    meta_go(7)
    meta_go(8)
    set_source(own.at[group], halves.at[group])
    add_source(lab_in, 0, 4, "first")
    have_meta(M2)
    meta_go(9)
    for i in (X1, X2, P0, P1, P3):
        have_meta(i)
    for i in (M1, M2, M3, X1, X2, P0, P1, P3):
        use_meta(i)
    arrive("o", 0)
    send("f", 0)
    arrive("x", 0)
    send("y", 0)
    mate_copies(1)
    send("h", 2)
    have_meta(P2)
    use_meta(P2)
    local(0, 2)
    source(0)
    add_source(xmeta.at[0], 0, 4, "add")
    arrive("o", 1)
    send("f", 1)
    arrive("x", 1)
    send("y", 1)
    source(2)
    add_source(xmeta.at[2], 0, 4, "add")
    arrive("o", 2)
    share(M1, 0, 6, 1)
    source(1)
    add_source(xmeta.at[1], 0, 2, "last")
    centroid_send(cores.at[other], from_core, 0, partner)
    add_source(xmeta.at[1], 2, 4, "last")
    landed(from_core, c_recv.at[0])
    for i in range(4):
        cores[core, i] = cores[core, i] + from_core[i]
    centroid_send(cores.at[core, ring(2), pl.ds(0, 2)], in_f, 1, forth)
    centroid_send(cores.at[core, ring(2), pl.ds(2, 2)], in_b, 2, back)
    send("f", 2)
    for i in range(9):
        list_copy(i).wait()
    shared_arrival(0)
    meet(None, P0, backward=False)
    meet(M1, P0, backward=False)
    meet(None, M1)
    arrive("x", 2)
    send("y", 2)
    arrive("f", 0)
    send("g", 0)
    meet(None, X1)
    meet(M1, X1)
    arrive("f", 1)
    send("g", 1)
    landed(in_b, c_recv.at[2])
    cores[core, ring(3), 2:4] = cores[core, ring(3), 2:4] + in_b[...]
    for k in SIDE_ORDER:
        centroid_send(cores.at[core, ring(3), across(k)], in2_b.at[across(k)], 24 + k, back)
    arrive("y", 0)
    landed(in_f, c_recv.at[1])
    cores[core, ring(1), 0:2] = cores[core, ring(1), 0:2] + in_f[...]
    for k in SIDE_ORDER:
        centroid_send(cores.at[core, ring(1), across(k)], in2_f.at[across(k)], 20 + k, forth)
    shared_arrival(1)
    meet(None, P1, backward=False)
    meet(M1, P1, backward=False)
    early = len(started) - 8
    arrive("f", 2)
    share(M2, 0, 6, 2)
    meet(None, M2, forward=False)
    meet(M2, X1)
    meet(M2, P0, backward=False)
    meet(M2, P1, backward=False)
    arrive("g", 0)
    share(M3, 0, 1, 4)
    arrive("y", 1)
    arrive("h", 2)
    share(M3, 3, 3, 3)
    shared_arrival(2)
    meet(None, P2, backward=False)
    meet(M1, P2, backward=False)
    meet(M2, P2, backward=False)
    drain(early)
    arrive("g", 1)
    share(M3, 1, 2, 5)
    meet(M3, X1)
    for i in (P0, P1, P2):
        meet(M3, i, backward=False)
    to_owners(1)
    to_owners(2)
    shared_arrival(3)
    for i in (M3, M2, M1, None):
        meet(i, P3, backward=False)
    for i in (P2, P1, P3, X1, P0):
        give_back(i)
    to_owners(3)
    arrive("y", 2)
    for i in (None, M1, M2, M3):
        meet(i, X2, forward=False)
    for i in (X2, M2, M1, M3):
        give_back(i)
    to_owners(0)
    drain(len(started) - 20)
    for i, k in owners:
        landed(in_last.at[i, k], c_recv.at[4 * i + k + 4])
    finish_centroids()
    stores = [pltpu.make_async_copy(src, dst, out_sem.at[i]) for i, (src, dst) in enumerate(
        ((centroids_out, centroids_hbm), (scores_out, scores_hbm)))]
    stores[0].start()
    drain(len(started))
    best = jnp.maximum(accs[9][...], 0.0)
    for i in range(9):
        landed(result_in.at[i], res_recv.at[i])
        best = jnp.maximum(best, result_in[i])
    scores_out[...] = best
    stores[1].start()
    for copy in stores:
        copy.wait()


def exchange(embeddings, labels, ranking, send_list, pair_list):
    dataset = pltpu.VMEM((SLICES, 4, BLOCK, LANES), jnp.bfloat16)
    dma = pltpu.SemaphoreType.DMA
    f32, bf16, i32 = jnp.float32, jnp.bfloat16, jnp.int32
    return pl.pallas_call(
        kernel,
        out_shape=(jax.ShapeDtypeStruct((8, LANES), f32), jax.ShapeDtypeStruct((32, SLICES * LANES), f32)),
        in_specs=[pl.BlockSpec(memory_space=pl.ANY)] * 5,
        out_specs=(pl.BlockSpec(memory_space=pl.ANY), pl.BlockSpec(memory_space=pl.ANY)),
        scratch_shapes=[dataset] * 10
        + [pltpu.VMEM((16, LANES), i32)] * 11
        + [pltpu.SMEM((8, LANES), i32)] * 10
        + [pltpu.VMEM((4, BLOCK, LANES), i32)] * 4
        + [pltpu.VMEM((8, LANES), f32)] * 10
        + [pltpu.VMEM((4, 8, BLOCK), i32)] * 10
        + [pltpu.VMEM((9, 8, LANES), f32),
           pltpu.VMEM((4, 2, BLOCK, LANES), bf16),
           pltpu.VMEM((3, 4, BLOCK, LANES), bf16),
           pltpu.VMEM((3, 2, BLOCK, LANES), bf16),
           pltpu.VMEM((3, 8, LANES), i32),
           pltpu.VMEM((ROWS, 2 * LANES), bf16),
           pltpu.VMEM((4, ROWS, 2 * LANES), f32),
           pltpu.VMEM((2, 4, 4, 4, 48, LANES), f32),
           pltpu.VMEM((4, 4, 4, 48, LANES), f32),
           pltpu.VMEM((2, 4, 48, LANES), f32),
           pltpu.VMEM((2, 4, 48, LANES), f32),
           pltpu.VMEM((4, 4, 48, LANES), f32),
           pltpu.VMEM((4, 4, 48, LANES), f32),
           pltpu.VMEM((4, 4, 48, LANES), f32),
           dma((18,)), dma((18,)), dma((6,)), dma((4,)),
           dma((10,)), dma((11,)), dma((10,)), dma((9,)), dma((9,)), dma((3, 3)), dma((3, 3)), dma((28,)), dma((28,)),
           pltpu.VMEM((ROWS, SLICES * LANES), bf16), pltpu.VMEM((8, LANES), i32), pltpu.VMEM((8, LANES), i32),
           pltpu.VMEM((1, 32), i32), pltpu.VMEM((1, 32), i32), dma((5,)),
           pltpu.VMEM((8, LANES), f32), pltpu.VMEM((32, SLICES * LANES), f32), dma((2,))],
        compiler_params=pltpu.CompilerParams(collective_id=0, has_side_effects=True, vmem_limit_bytes=60 * 1024 * 1024),
    )(embeddings, labels.reshape(8, LANES), ranking.reshape(8, LANES), send_list, pair_list)


def store_kernel(scores_in, centroids_in, scores_out, centroids_out):
    scores_out[...] = jnp.maximum(scores_in[...], 0.0)
    centroids_out[...] = centroids_in[...]


def store(scores, centroids):
    return pl.pallas_call(
        store_kernel,
        out_shape=(jax.ShapeDtypeStruct(scores.shape, scores.dtype), jax.ShapeDtypeStruct(centroids.shape, centroids.dtype)),
        in_specs=[pl.BlockSpec(memory_space=pltpu.VMEM)] * 2,
        out_specs=(pl.BlockSpec(memory_space=pltpu.VMEM), pl.BlockSpec(memory_space=pltpu.VMEM)),
    )(scores, centroids)


def body(embeddings, labels, ranking, send_list, pair_list):
    scores, centroids = exchange(embeddings, labels, ranking, send_list, pair_list)
    scores, centroids = store(scores, centroids)
    return (scores.reshape(ROWS), centroids)


def solution(mesh):
    return jax.shard_map(
        body,
        mesh=mesh,
        in_specs=(
            P(("group", "dev"), None),
            P(("group", "dev")),
            P(("group", "dev")),
            P(("group", "dev"), None),
            P(("group", "dev"), None),
        ),
        out_specs=(P(("group", "dev")), P(("group", "dev"), None)),
        check_vma=False,
    )
```
